32 devices in a mesh: fsdp: 4 (over y, x), seq: 8 (over z, core).
Axes of the slice: x: 2, y: 2, z: 4, core: 2. Of those that a mesh axis runs over, the one named last changes fastest.
Arguments:
- tokens: bfloat16 [4, 1024, 2048], P('fsdp', 'seq'), may hold values from -6 to 6
- teacher: bfloat16 [4, 1024, 2048], P('fsdp', 'seq'), may hold values from -6 to 6
- segments: int32 [4, 1024], P('fsdp', 'seq'), may hold values from 0 to 255, as said below
- valid: int32 [4, 1024], P('fsdp', 'seq'), may hold values from 0 to 1, as said below
- query_weight: bfloat16 [2048, 2048], P(('fsdp', 'seq')), may hold values from -0.125 to 0.125
- key_weight: bfloat16 [2048, 2048], P(('fsdp', 'seq')), may hold values from -0.125 to 0.125
- value_weight: bfloat16 [2048, 2048], P(('fsdp', 'seq')), may hold values from -0.125 to 0.125
- output_weight: bfloat16 [2048, 2048], P(('fsdp', 'seq')), may hold values from -0.5 to 0.5
- attention_gain: bfloat16 [2048], P(('fsdp', 'seq')), may hold values from 0.25 to 1.75
- gate_weight: bfloat16 [2048, 8192], P(('fsdp', 'seq')), may hold values from -0.125 to 0.125
- up_weight: bfloat16 [2048, 8192], P(('fsdp', 'seq')), may hold values from -0.125 to 0.125
- down_weight: bfloat16 [8192, 2048], P(('fsdp', 'seq')), may hold values from -0.125 to 0.125
- mlp_gain: bfloat16 [2048], P(('fsdp', 'seq')), may hold values from 0.25 to 1.75
Outputs:
- output: bfloat16 [4, 1024, 2048], P('fsdp', 'seq')
- loss: float32 [], replicated
- input_grad: float32 [4, 1024, 2048], P('fsdp', 'seq')
- query_weight_grad: float32 [2048, 2048], P(('fsdp', 'seq'))
- key_weight_grad: float32 [2048, 2048], P(('fsdp', 'seq'))
- value_weight_grad: float32 [2048, 2048], P(('fsdp', 'seq'))
- output_weight_grad: float32 [2048, 2048], P(('fsdp', 'seq'))
- attention_gain_grad: float32 [2048], P(('fsdp', 'seq'))
- gate_weight_grad: float32 [2048, 8192], P(('fsdp', 'seq'))
- up_weight_grad: float32 [2048, 8192], P(('fsdp', 'seq'))
- down_weight_grad: float32 [8192, 2048], P(('fsdp', 'seq'))
- mlp_gain_grad: float32 [2048], P(('fsdp', 'seq'))
The draws below stay inside these ranges and needn't reach their ends.
Inputs may be any that keep to these rules, and one draw needn't show every extreme that they name: `segments`: within a sequence the document numbers start at 0 and never fall, and a document begins only at a place that is a multiple of 4; when an index of fsdp holds two or more sequences, one of them is a single document (with one sequence per index, as here, this does not occur). The first token of every sequence is valid.
All inputs are finite; a program needn't handle non-finite values.
Results may differ from the reference program's by a relative error of at most 0.012.
The reference program's roundings to bfloat16 on the way count: a program that leaves them out, or rounds other values in their place, can miss the bound.
Values may be sent and summed in bfloat16 or wider, within the bound.
No kernel may reach another device: no remote copies, remote signals or barrier semaphores. Data moves between devices by JAX's collectives and lax.ppermute only.
A program may use at most 640 MiB of HBM per device.

```python
import jax
import jax.numpy as jnp
from jax import lax

D = 2048
H = 32
HD = 64
FF = 8192
SEQS = 1
SEQ_LEN = 1024
NSEQ = 4


def draw_segments(key, part):
    key = jax.random.fold_in(key, 11)
    span_key, flag_key, pick_key = jax.random.split(key, 3)
    longest = max(SEQ_LEN.bit_length() - 1, 3)
    span_bits = jax.random.randint(span_key, (NSEQ, 1), 2, longest + 1)
    period = jnp.left_shift(jnp.ones_like(span_bits), span_bits - 2)
    random_bits = jax.random.randint(flag_key, (NSEQ, SEQ_LEN), 0, 1 << 20)
    column = jnp.arange(SEQ_LEN, dtype=jnp.int32)[None, :]
    group_count = NSEQ // SEQS
    chosen = jax.random.randint(pick_key, (group_count, 1), 0, SEQS)
    member = jnp.arange(SEQS, dtype=jnp.int32)[None, :]
    single = ((member == chosen) & (SEQS > 1)).reshape(NSEQ)
    densest = (member == (chosen + 1) % SEQS).reshape(NSEQ)
    first_group = jnp.arange(NSEQ, dtype=jnp.int32) < SEQS
    dense_row = (densest & first_group & jnp.logical_not(single))[:, None]
    quarter = (column % 4 == 0) & (column > 0)
    flagged = (random_bits % period == 0) | dense_row
    starts = (quarter & flagged).astype(jnp.int32)
    numbers = jnp.cumsum(starts, axis=1).astype(jnp.int32)
    return jnp.where(single[:, None], 0, numbers).astype(jnp.int32)


def draw_valid(key, part):
    key = jax.random.fold_in(key, 23)
    all_tokens = NSEQ * SEQ_LEN
    places = jnp.arange(all_tokens, dtype=jnp.int32).reshape(NSEQ, SEQ_LEN)
    limits = 250 + 700 * places // all_tokens
    limits = jnp.where(places % SEQ_LEN == 0, 1000, limits)
    random_draws = jax.random.randint(key, (NSEQ, SEQ_LEN), 0, 1000)
    return (random_draws < limits).astype(jnp.int32)


def levels(own_key, extent, pieces, low, top_value):
    gain, own = 1.0, jax.random.fold_in(own_key, 6)
    for dim, shards_of in pieces:
        draws = jnp.exp(jax.random.uniform(jax.random.fold_in(own, dim), (shards_of,), jnp.float32, low / len(pieces), top_value / len(pieces)))
        gain = gain * jnp.repeat(draws, extent[dim] // shards_of).reshape([-1 if axis == dim else 1 for axis in range(len(extent))])
    return gain


def scatter_about(own_key, shape, spread, limit, shards=(), kind=jnp.bfloat16):
    level = levels(own_key, shape, shards, -0.22, 0.18) if shards else 1.0
    values = jax.random.normal(own_key, shape, jnp.float32) * spread * level
    return jnp.minimum(jnp.maximum(values, -limit), limit).astype(kind)


def setup_inputs(seed: int = 0) -> dict:
    arg_keys = jax.random.split(jax.random.key(seed), 14)
    return {
        "tokens": scatter_about(arg_keys[0], (NSEQ, SEQ_LEN, D), 1.0, 6.0, ((0, 4), (1, 8))),
        "teacher": scatter_about(arg_keys[1], (NSEQ, SEQ_LEN, D), 1.0, 6.0, ((0, 4), (1, 8))),
        "segments": draw_segments(jax.random.fold_in(arg_keys[13], 71), 0),
        "valid": draw_valid(jax.random.fold_in(arg_keys[13], 71), 0),
        "query_weight": scatter_about(arg_keys[4], (D, D), D ** -0.5, 0.125, ((0, 32),)),
        "key_weight": scatter_about(arg_keys[5], (D, D), D ** -0.5, 0.125, ((0, 32),)),
        "value_weight": scatter_about(arg_keys[6], (D, D), D ** -0.5, 0.125, ((0, 32),)),
        "output_weight": scatter_about(arg_keys[7], (D, D), (D // 16) ** -0.5, 0.5, ((0, 32),)),
        "attention_gain": jnp.clip(1.0 + 0.15 * jax.random.normal(arg_keys[8], (D,), jnp.float32), 0.25, 1.75).astype(jnp.bfloat16),
        "gate_weight": scatter_about(arg_keys[9], (D, FF), D ** -0.5, 0.125, ((0, 32),)),
        "up_weight": scatter_about(arg_keys[10], (D, FF), D ** -0.5, 0.125, ((0, 32),)),
        "down_weight": scatter_about(arg_keys[11], (FF, D), (FF // 4) ** -0.5, 0.125, ((0, 32),)),
        "mlp_gain": jnp.clip(1.0 + 0.15 * jax.random.normal(arg_keys[12], (D,), jnp.float32), 0.25, 1.75).astype(jnp.bfloat16),
    }


@jax.custom_vjp
def low(v):
    return lax.optimization_barrier(v.astype(jnp.bfloat16)).astype(jnp.float32)

@jax.custom_vjp
def low_back(v):
    return v

def low_keep(v):
    return (low(v), None)

def low_pass(kept, grad):
    return (grad,)

def back_keep(v):
    return (v, None)

def back_low(kept, grad):
    return (low(grad),)
low.defvjp(low_keep, low_pass)
low_back.defvjp(back_keep, back_low)
EPSILON = 1e-05
ROPE_BASE = 130000.0
MASKED = -1e+30
HIGHEST = lax.Precision.HIGHEST

def product(left_side, right_side):
    return jnp.dot(left_side, right_side, precision=HIGHEST, preferred_element_type=jnp.float32)

def rms_norm(values, gain_vector):
    return values * lax.rsqrt(lax.optimization_barrier(jnp.mean(values * values, axis=-1, keepdims=True)) + EPSILON) * gain_vector

def rotate(values, positions):
    half_width = values.shape[-1] // 2
    exponents = jnp.arange(half_width).astype(jnp.float32) * (2.0 / values.shape[-1])
    inverse = jnp.power(ROPE_BASE, -exponents)
    angles = positions[:, None] * inverse[None, :]
    cosine = jnp.cos(angles)[:, None, :]
    sine_part = jnp.sin(angles)[:, None, :]
    leading = values[..., :half_width]
    trailing = values[..., half_width:]
    return jnp.concatenate([leading * cosine - trailing * sine_part, trailing * cosine + leading * sine_part], axis=-1)

def attention(query_heads, key_heads, value_heads, segment):
    block_rows = min(512, SEQ_LEN)
    key_places = jnp.arange(SEQ_LEN).astype(jnp.int32)
    score_scale = HD ** (-0.5)

    def one_block(first_row):
        query_rows = lax.dynamic_slice_in_dim(query_heads, first_row, block_rows, 0)
        segment_rows = lax.dynamic_slice_in_dim(segment, first_row, block_rows, 0)
        row_places = first_row + jnp.arange(block_rows).astype(jnp.int32)
        allowed = (segment_rows[:, None] == segment[None, :]) & (key_places[None, :] <= row_places[:, None])
        scores = low_back(jnp.einsum('qhd,khd->hqk', query_rows, key_heads, precision=HIGHEST) * score_scale)
        scores = jnp.where(allowed[None], scores, MASKED)
        row_max = lax.optimization_barrier(jnp.max(scores, axis=-1, keepdims=True))
        exponent = jnp.exp(scores - row_max)
        weights = low(exponent / lax.optimization_barrier(jnp.sum(exponent, axis=-1, keepdims=True)))
        return jnp.einsum('hqk,khd->qhd', weights, value_heads, precision=HIGHEST)
    block_starts = (jnp.arange(SEQ_LEN // block_rows) * block_rows).astype(jnp.int32)
    result = lax.map(jax.checkpoint(one_block), block_starts)
    return result.reshape(SEQ_LEN, H * HD)

def layer(inputs, segment, query_weight, key_weight, value_weight, output_weight, attention_gain, gate_weight, up_weight, down_weight, mlp_gain):
    normed = low(rms_norm(inputs, attention_gain))
    positions = jnp.arange(SEQ_LEN).astype(jnp.float32)
    head_shape = (SEQ_LEN, H, HD)
    query_heads = low_back(low(rotate(low_back(product(normed, query_weight)).reshape(head_shape), positions)))
    key_heads = low_back(low(rotate(low_back(product(normed, key_weight)).reshape(head_shape), positions)))
    value_heads = low_back(low(product(normed, value_weight))).reshape(head_shape)
    mixed = low_back(low(attention(query_heads, key_heads, value_heads, segment)))
    after_attention = inputs + low_back(product(mixed, output_weight))
    normed_two = low(rms_norm(after_attention, mlp_gain))
    gate_value = low_back(product(normed_two, gate_weight))
    up_value = low_back(product(normed_two, up_weight))
    hidden = low(gate_value * jax.nn.sigmoid(gate_value) * up_value)
    return after_attention + low_back(product(hidden, down_weight))

def reference(tokens, teacher, segments, valid, query_weight, key_weight, value_weight, output_weight, attention_gain, gate_weight, up_weight, down_weight, mlp_gain):
    params = tuple((array.astype(jnp.float32) for array in (query_weight, key_weight, value_weight, output_weight, attention_gain, gate_weight, up_weight, down_weight, mlp_gain)))
    count = jnp.sum(valid.astype(jnp.float32))

    def per_sequence(running, element):
        inputs, target, segment, keep_mask = element

        def forward(layer_input, *weight_list):
            result = layer(layer_input, segment, *weight_list)
            difference = result - target.astype(jnp.float32)
            return (result, jnp.sum(keep_mask.astype(jnp.float32)[:, None] * difference * difference) / count)
        (result, loss_part), pullback = jax.vjp(forward, inputs.astype(jnp.float32), *params)
        gradients = pullback((jnp.zeros_like(result), jnp.ones_like(loss_part)))
        loss_total, grad_sums = running
        grad_sums = tuple((total_grad + new_grad for total_grad, new_grad in zip(grad_sums, gradients[1:])))
        return ((loss_total + loss_part, grad_sums), (result.astype(jnp.bfloat16), gradients[0]))
    initial = (jnp.zeros((), jnp.float32), tuple((jnp.zeros_like(array) for array in params)))
    (loss, grad_sums), (output, input_grad) = lax.scan(per_sequence, initial, (tokens, teacher, segments, valid))
    return (output, loss, input_grad, grad_sums[0], grad_sums[1], grad_sums[2], grad_sums[3], grad_sums[4], grad_sums[5], grad_sums[6], grad_sums[7], grad_sums[8])
```

```python
import jax
import jax.numpy as jnp
from jax import lax
from jax.sharding import PartitionSpec as P

H = 32
HD = 64
EPSILON = 1e-05
ROPE_BASE = 130000.0
MASKED = -1e30
BF = jnp.bfloat16
F32 = jnp.float32
ALL = ("fsdp", "seq")


def rms_norm(values, gain_vector):
    return (
        values
        * lax.rsqrt(jnp.mean(values * values, axis=-1, keepdims=True) + EPSILON)
        * gain_vector
    )


def rope_tables(length):
    exponents = jnp.arange(HD // 2).astype(F32) * (2.0 / HD)
    inverse = jnp.power(ROPE_BASE, -exponents)
    angles = jnp.arange(length, dtype=jnp.int32).astype(F32)[:, None] * inverse[None, :]
    return jnp.cos(angles), jnp.sin(angles)


def rotate(values, cosine, sine):
    half = HD // 2
    cosine, sine = cosine[:, None, :], sine[:, None, :]
    leading, trailing = values[..., :half], values[..., half:]
    return jnp.concatenate(
        [leading * cosine - trailing * sine, trailing * cosine + leading * sine], axis=-1
    )


def matmul(left_side, right_side):
    return jnp.dot(left_side, right_side, preferred_element_type=F32)


def transposed(left_side, right_side):
    return lax.dot_general(
        left_side, right_side, (((0,), (0,)), ((), ())), preferred_element_type=F32
    )


def against(left_side, right_side):
    return lax.dot_general(
        left_side, right_side, (((1,), (1,)), ((), ())), preferred_element_type=F32
    )


def gated(gate_value, up_value):
    return gate_value * jax.nn.sigmoid(gate_value) * up_value


def gather_rows(local):
    return lax.all_gather(local, "seq", axis=0, tiled=True)


def scatter_rows(partial):
    return lax.psum_scatter(
        partial.astype(BF), "seq", scatter_dimension=0, tiled=True
    ).astype(F32)


def columns_in(weight, blocks):
    groups = lax.axis_size("seq")
    rows, width = weight.shape
    part = width // (blocks * groups)
    swapped = lax.all_to_all(
        weight.reshape(rows, blocks, groups, part), "seq", split_axis=2, concat_axis=0, tiled=True
    ).reshape(groups * rows, blocks * part)
    return lax.all_gather(swapped, "fsdp", axis=0, tiled=True)


def columns_out(grad, blocks):
    groups = lax.axis_size("seq")
    part = grad.shape[1] // blocks
    summed = lax.psum_scatter(grad.astype(BF), "fsdp", scatter_dimension=0, tiled=True)
    rows = summed.shape[0] // groups
    swapped = lax.all_to_all(
        summed.reshape(groups * rows, blocks, 1, part),
        "seq",
        split_axis=0,
        concat_axis=2,
        tiled=True,
    )
    return swapped.reshape(rows, blocks * groups * part).astype(F32)


def rows_in(weight):
    return lax.all_gather(weight, "fsdp", axis=0, tiled=True)


def rows_out(grad):
    return lax.psum_scatter(
        grad.astype(BF), "fsdp", scatter_dimension=0, tiled=True
    ).astype(F32)


def body(
    tokens,
    teacher,
    segments,
    valid,
    query_weight,
    key_weight,
    value_weight,
    output_weight,
    attention_gain,
    gate_weight,
    up_weight,
    down_weight,
    mlp_gain,
):
    sequences, local_rows, width = tokens.shape
    groups = lax.axis_size("seq")
    shards = lax.axis_size("fsdp")
    heads = H // groups
    length = local_rows * groups
    scale = HD ** (-0.5)
    own = lax.axis_index("seq")
    aligned = H % (shards * groups) == 0
    head_blocks = shards if aligned else 1

    inputs = tokens.reshape(local_rows, width).astype(F32)
    tokens_all = gather_rows(tokens.reshape(local_rows, width)).astype(F32)
    segment = lax.all_gather(segments, "seq", axis=1, tiled=True).reshape(length)
    gains = lax.all_gather(
        jnp.stack([attention_gain, mlp_gain], axis=1), ALL, axis=0, tiled=True
    ).astype(F32)
    first_gain, second_gain = gains[:, 0], gains[:, 1]
    normed = rms_norm(tokens_all, first_gain).astype(BF)

    qkv_weight = jnp.concatenate(
        [columns_in(w, head_blocks) for w in (query_weight, key_weight, value_weight)], axis=1
    )
    if aligned:
        out_weight = rows_in(output_weight)
    else:
        out_weight = lax.dynamic_slice_in_dim(
            lax.all_gather(output_weight, ALL, axis=0, tiled=True),
            own * heads * HD,
            heads * HD,
            0,
        )
    gate_up_weight = jnp.concatenate(
        [columns_in(gate_weight, shards), columns_in(up_weight, shards)], axis=1
    )
    down_full = rows_in(down_weight)

    hw = heads * HD
    qkv = matmul(normed, qkv_weight)
    cosine, sine = rope_tables(length)

    def rotated(values):
        return rotate(values.reshape(length, heads, HD), cosine, sine)

    query = rotated(qkv[:, :hw]).astype(BF)
    key = rotated(qkv[:, hw : 2 * hw]).astype(BF)
    value = qkv[:, 2 * hw :].astype(BF).reshape(length, heads, HD)
    places = jnp.arange(length, dtype=jnp.int32)
    allowed = (segment[:, None] == segment[None, :]) & (places[None, :] <= places[:, None])
    scores = jnp.einsum("qhd,khd->hqk", query, key, preferred_element_type=F32) * scale
    scores = jnp.where(allowed[None], scores, MASKED)
    row_max = jnp.max(scores, axis=-1, keepdims=True)
    exponent = jnp.exp(scores - row_max)
    row_total = jnp.sum(exponent, axis=-1, keepdims=True)
    probs = exponent / row_total
    weights = probs.astype(BF)
    mixed = (
        jnp.einsum("hqk,khd->qhd", weights, value, preferred_element_type=F32)
        .astype(BF)
        .reshape(length, hw)
    )
    after_attention = inputs + scatter_rows(matmul(mixed, out_weight))
    normed_two_own = rms_norm(after_attention, second_gain).astype(BF)
    normed_two = gather_rows(normed_two_own)
    gate_up = matmul(normed_two, gate_up_weight)
    hidden_width = gate_up.shape[1] // 2
    gate_value, up_value = gate_up[:, :hidden_width], gate_up[:, hidden_width:]
    hidden = gated(gate_value, up_value).astype(BF)
    result = after_attention + scatter_rows(matmul(hidden, down_full))
    keep_mask = valid.reshape(local_rows).astype(F32)
    difference = result - teacher.reshape(local_rows, width).astype(F32)
    count, error_sum = lax.psum(
        (jnp.sum(keep_mask), jnp.sum(keep_mask[:, None] * difference * difference)), ALL
    )
    loss = error_sum / count
    grad_result = 2.0 / count * keep_mask[:, None] * difference
    grad_branch = gather_rows(grad_result.astype(BF))
    grad_hidden = against(grad_branch, down_full)
    unused, gate_pull = jax.vjp(gated, gate_value, up_value)
    grad_gate, grad_upward = gate_pull(grad_hidden)
    gate_up_grad = jnp.concatenate([grad_gate.astype(BF), grad_upward.astype(BF)], axis=1)
    grad_normed_two = scatter_rows(against(gate_up_grad, gate_up_weight))
    unused, second_pull = jax.vjp(rms_norm, after_attention, second_gain)
    grad_after, second_gain_grad = second_pull(grad_normed_two)
    grad_after = grad_after + grad_result
    down_sum = rows_out(transposed(hidden, grad_branch))
    gate_up_weight_grad = transposed(normed_two, gate_up_grad)
    gate_sum = columns_out(gate_up_weight_grad[:, :hidden_width], shards)
    up_sum = columns_out(gate_up_weight_grad[:, hidden_width:], shards)

    grad_out = gather_rows(grad_after.astype(BF))
    grad_mixed = against(grad_out, out_weight).astype(BF).reshape(length, heads, HD)
    output_grad = transposed(mixed, grad_out)
    if aligned:
        output_sum = rows_out(output_grad)
    else:
        output_sum = lax.psum_scatter(
            lax.dynamic_update_slice_in_dim(
                jnp.zeros((width, width), BF), output_grad.astype(BF), own * hw, 0
            ),
            ALL,
            scatter_dimension=0,
            tiled=True,
        ).astype(F32)
    grad_probs = jnp.einsum("qhd,khd->hqk", grad_mixed, value, preferred_element_type=F32)
    inner = jnp.sum(probs * grad_probs, axis=-1, keepdims=True)
    grad_scores = (probs * (grad_probs - inner)).astype(BF)
    grad_query = (
        jnp.einsum("hqk,khd->qhd", grad_scores, key, preferred_element_type=F32) * scale
    ).astype(BF)
    grad_key = (
        jnp.einsum("hqk,qhd->khd", grad_scores, query, preferred_element_type=F32) * scale
    ).astype(BF)
    grad_value = jnp.einsum("hqk,qhd->khd", weights, grad_mixed, preferred_element_type=F32)

    def rotated_back(values):
        return rotate(values.astype(F32), cosine, -sine).astype(BF).reshape(length, hw)

    qkv_grad = jnp.concatenate(
        [
            rotated_back(grad_query),
            rotated_back(grad_key),
            grad_value.astype(BF).reshape(length, hw),
        ],
        axis=1,
    )
    grad_normed = scatter_rows(against(qkv_grad, qkv_weight))
    unused, first_pull = jax.vjp(rms_norm, inputs, first_gain)
    grad_inputs, first_gain_grad = first_pull(grad_normed)
    grad_inputs = grad_inputs + grad_after
    qkv_weight_grad = transposed(normed, qkv_grad)
    query_sum, key_sum, value_sum = (
        columns_out(qkv_weight_grad[:, i * hw : (i + 1) * hw], head_blocks) for i in range(3)
    )
    gain_sums = lax.psum_scatter(
        jnp.stack([first_gain_grad, second_gain_grad], axis=1),
        ALL,
        scatter_dimension=0,
        tiled=True,
    )
    output_shape = (sequences, local_rows, width)
    return (
        result.reshape(output_shape).astype(BF),
        loss,
        grad_inputs.reshape(output_shape),
        query_sum,
        key_sum,
        value_sum,
        output_sum,
        gain_sums[:, 0],
        gate_sum,
        up_sum,
        down_sum,
        gain_sums[:, 1],
    )


def solution(mesh):
    rows = P("fsdp", "seq", None)
    places = P("fsdp", "seq")
    matrix = P(ALL, None)
    vector = P(ALL)
    return jax.shard_map(
        body,
        mesh=mesh,
        in_specs=(
            rows,
            rows,
            places,
            places,
            matrix,
            matrix,
            matrix,
            matrix,
            vector,
            matrix,
            matrix,
            matrix,
            vector,
        ),
        out_specs=(
            rows,
            P(),
            rows,
            matrix,
            matrix,
            matrix,
            matrix,
            vector,
            matrix,
            matrix,
            matrix,
            vector,
        ),
        check_vma=False,
    )
```

```python
import jax
import jax.numpy as jnp
from jax import lax
from jax.sharding import PartitionSpec as P

H = 32
HD = 64
EPSILON = 1e-05
ROPE_BASE = 130000.0
MASKED = -1e30
BF = jnp.bfloat16
F32 = jnp.float32
ALL = ("fsdp", "seq")


def rms_norm(values, gain_vector):
    return (
        values
        * lax.rsqrt(jnp.mean(values * values, axis=-1, keepdims=True) + EPSILON)
        * gain_vector
    )


def rope_tables(places):
    exponents = jnp.arange(HD // 2).astype(F32) * (2.0 / HD)
    inverse = jnp.power(ROPE_BASE, -exponents)
    angles = places.astype(F32)[:, None] * inverse[None, :]
    return jnp.cos(angles), jnp.sin(angles)


def rotate(values, cosine, sine):
    half = HD // 2
    cosine, sine = cosine[:, None, :], sine[:, None, :]
    leading, trailing = values[..., :half], values[..., half:]
    return jnp.concatenate(
        [leading * cosine - trailing * sine, trailing * cosine + leading * sine], axis=-1
    )


def matmul(left_side, right_side):
    return jnp.dot(left_side, right_side, preferred_element_type=F32)


def transposed(left_side, right_side):
    return lax.dot_general(
        left_side, right_side, (((0,), (0,)), ((), ())), preferred_element_type=F32
    )


def against(left_side, right_side):
    return lax.dot_general(
        left_side, right_side, (((1,), (1,)), ((), ())), preferred_element_type=F32
    )


def gated(gate_value, up_value):
    return gate_value * jax.nn.sigmoid(gate_value) * up_value


def turn(value, steps):
    size = lax.axis_size("seq")
    return lax.ppermute(value, "seq", [(s, (s - 2 * steps) % size) for s in range(size)])


def swap(value):
    return lax.ppermute(value, "seq", [(s, s ^ 1) for s in range(lax.axis_size("seq"))])


def place():
    own = lax.axis_index("seq")
    return own // 2, own % 2, lax.axis_size("seq") // 2


def order(chips):
    near = []
    for step in range(1, chips // 2 + 1):
        near += [step] if 2 * step == chips else [step, chips - step]
    return near


def gather_rows(local):
    chip, core, chips = place()
    parts = {0: local}
    for step in order(chips):
        parts[step] = turn(local, step)
    mine = [parts[step] for step in range(chips)]
    return jnp.concatenate(mine + [swap(part) for part in mine], axis=0)


def scatter_rows(left_side, weight, product):
    chip, core, chips = place()
    half = left_side.shape[0] // 2
    rows = half // chips
    other = swap(product(left_side[half:], weight).astype(BF))
    total = product(left_side[:half], weight) + other.astype(F32)
    parts = total.astype(BF)
    result = total[:rows]
    for step in order(chips):
        result = result + turn(parts[step * rows : (step + 1) * rows], -step).astype(F32)
    return result


def unroll(parts):
    chip, core, chips = place()
    return lax.dynamic_slice_in_dim(
        jnp.concatenate([parts, parts], axis=0), (chips - chip) % chips, chips, 0
    )


def by_core(mine, other, axis):
    chip, core, chips = place()
    return jnp.where(
        core == 0, jnp.stack([mine, other], axis=axis), jnp.stack([other, mine], axis=axis)
    )


def columns_in(weight):
    chip, core, chips = place()
    rows, groups, cols = weight.shape
    pairs = weight.reshape(rows, chips, 2 * cols)

    def share(step):
        return lax.dynamic_index_in_dim(pairs, (chip + step) % chips, 1, keepdims=False)

    parts = {0: share(0)}
    for step in order(chips):
        parts[chips - step] = turn(share(step), -step)
    stacked = unroll(jnp.stack([parts[step] for step in range(chips)])).reshape(
        chips, rows, 2, cols
    )
    mine = lax.dynamic_index_in_dim(stacked, core, 2, keepdims=False)
    other = swap(lax.dynamic_index_in_dim(stacked, 1 - core, 2, keepdims=False))
    local = by_core(mine, other, 1).reshape(groups * rows, cols)
    return lax.all_gather(local, "fsdp", axis=0, tiled=True)


def columns_out(grad):
    chip, core, chips = place()
    cols = grad.shape[1]
    summed = lax.psum_scatter(grad.astype(BF), "fsdp", scatter_dimension=0, tiled=True)
    rows = summed.shape[0] // (2 * chips)
    stacked = summed.reshape(chips, 2, rows, cols)
    mine = lax.dynamic_index_in_dim(stacked, core, 1, keepdims=False)
    other = swap(lax.dynamic_index_in_dim(stacked, 1 - core, 1, keepdims=False))
    pairs = by_core(mine, other, 2)

    def share(step):
        return lax.dynamic_index_in_dim(pairs, (chip + step) % chips, 0, keepdims=False)

    parts = {0: share(0)}
    for step in order(chips):
        parts[chips - step] = turn(share(step), -step)
    natural = unroll(jnp.stack([parts[step] for step in range(chips)]))
    return jnp.moveaxis(natural, 0, 1).reshape(rows, 2 * chips, cols)


def rows_in(weight):
    return lax.all_gather(weight, "fsdp", axis=0, tiled=True)


def rows_out(grad):
    return lax.psum_scatter(
        grad.astype(BF), "fsdp", scatter_dimension=0, tiled=True
    ).astype(F32)


def sum_to_owners(values):
    for axis in ALL:
        size, own = lax.axis_size(axis), lax.axis_index(axis)
        bit = size // 2
        while bit:
            halves = values.reshape(2, values.shape[0] // 2, values.shape[1])
            mine = (own // bit) % 2
            keep = lax.dynamic_index_in_dim(halves, mine, 0, keepdims=False)
            give = lax.dynamic_index_in_dim(halves, 1 - mine, 0, keepdims=False)
            values = keep + lax.ppermute(give, axis, [(s, s ^ bit) for s in range(size)])
            bit //= 2
    return values[0]


def split_columns(weight, blocks):
    groups = lax.axis_size("seq")
    rows, width = weight.shape
    return jnp.moveaxis(
        weight.reshape(rows, blocks, groups, width // (blocks * groups)), 1, 2
    ).reshape(rows, groups, width // groups)


def join_columns(weight, blocks):
    rows, groups, cols = weight.shape
    return (
        jnp.moveaxis(weight.reshape(rows, groups, blocks, cols // blocks), 2, 1)
        .reshape(rows, groups * cols)
        .astype(F32)
    )


def body(
    tokens,
    teacher,
    segments,
    valid,
    query_weight,
    key_weight,
    value_weight,
    output_weight,
    attention_gain,
    gate_weight,
    up_weight,
    down_weight,
    mlp_gain,
):
    sequences, local_rows, width = tokens.shape
    groups = lax.axis_size("seq")
    shards = lax.axis_size("fsdp")
    heads = H // groups
    length = local_rows * groups
    scale = HD ** (-0.5)
    own = lax.axis_index("seq")
    chip, core, chips = place()
    weight_rows = query_weight.shape[0]
    aligned = H % (shards * groups) == 0
    head_blocks = shards if aligned else 1
    hw = heads * HD

    inputs = tokens.reshape(local_rows, width).astype(F32)
    keep_mask = valid.reshape(local_rows).astype(F32)
    spread = local_rows // weight_rows
    own_segments = segments.reshape(weight_rows, spread)
    extra = jnp.concatenate(
        [
            attention_gain[:, None],
            mlp_gain[:, None],
            jnp.full((weight_rows, 1), jnp.sum(keep_mask)).astype(BF),
            (own_segments // 256).astype(BF),
            (own_segments % 256).astype(BF),
        ],
        axis=1,
    )
    extra = jnp.pad(extra, ((0, 0), (0, 128 - extra.shape[1])))
    attention_in = columns_in(
        jnp.concatenate(
            [split_columns(w, head_blocks) for w in (query_weight, key_weight, value_weight)]
            + [jnp.broadcast_to(extra[:, None], (weight_rows, groups, 128))],
            axis=2,
        )
    )
    qkv_weight = attention_in[:, : 3 * hw]
    extras = attention_in[:, 3 * hw :].astype(F32)
    first_gain, second_gain = extras[:, 0], extras[:, 1]
    count = jnp.sum(extras[::weight_rows, 2])
    table = lax.dynamic_slice_in_dim(
        extras, lax.axis_index("fsdp") * groups * weight_rows, groups * weight_rows, 0
    ).astype(jnp.int32)
    segment_blocks = (table[:, 3 : 3 + spread] * 256 + table[:, 3 + spread : 3 + 2 * spread]).reshape(
        groups, local_rows
    )
    relative = jnp.arange(groups, dtype=jnp.int32)
    block_of = (chip + relative % chips) % chips * 2 + (core + relative // chips) % 2
    segment = segment_blocks[block_of].reshape(length)
    places = (
        block_of[:, None] * local_rows + jnp.arange(local_rows, dtype=jnp.int32)[None, :]
    ).reshape(length)

    tokens_all = gather_rows(tokens.reshape(local_rows, width)).astype(F32)
    normed = rms_norm(tokens_all, first_gain).astype(BF)
    if aligned:
        out_weight = rows_in(output_weight)
    else:
        out_weight = lax.dynamic_slice_in_dim(
            lax.all_gather(output_weight, ALL, axis=0, tiled=True), own * hw, hw, 0
        )
    gate_up_weight = columns_in(
        jnp.concatenate(
            [split_columns(gate_weight, shards), split_columns(up_weight, shards)], axis=2
        )
    )
    down_full = rows_in(down_weight)

    qkv = matmul(normed, qkv_weight)
    cosine, sine = rope_tables(places)

    def rotated(values):
        return rotate(values.reshape(length, heads, HD), cosine, sine)

    query = rotated(qkv[:, :hw]).astype(BF)
    key = rotated(qkv[:, hw : 2 * hw]).astype(BF)
    value = qkv[:, 2 * hw :].astype(BF).reshape(length, heads, HD)
    allowed = (segment[:, None] == segment[None, :]) & (places[None, :] <= places[:, None])
    scores = jnp.einsum("qhd,khd->hqk", query, key, preferred_element_type=F32) * scale
    scores = jnp.where(allowed[None], scores, MASKED)
    row_max = jnp.max(scores, axis=-1, keepdims=True)
    exponent = jnp.exp(scores - row_max)
    row_total = jnp.sum(exponent, axis=-1, keepdims=True)
    probs = exponent / row_total
    weights = probs.astype(BF)
    mixed = (
        jnp.einsum("hqk,khd->qhd", weights, value, preferred_element_type=F32)
        .astype(BF)
        .reshape(length, hw)
    )
    after_attention = inputs + scatter_rows(mixed, out_weight, matmul)
    normed_two = gather_rows(rms_norm(after_attention, second_gain).astype(BF))
    gate_up = matmul(normed_two, gate_up_weight)
    hidden_width = gate_up.shape[1] // 2
    gate_value, up_value = gate_up[:, :hidden_width], gate_up[:, hidden_width:]
    hidden = gated(gate_value, up_value).astype(BF)
    result = after_attention + scatter_rows(hidden, down_full, matmul)
    difference = result - teacher.reshape(local_rows, width).astype(F32)
    error_sum = jnp.sum(keep_mask[:, None] * difference * difference)
    grad_result = 2.0 / count * keep_mask[:, None] * difference
    grad_branch = gather_rows(grad_result.astype(BF))
    grad_hidden = against(grad_branch, down_full)
    unused, gate_pull = jax.vjp(gated, gate_value, up_value)
    grad_gate, grad_upward = gate_pull(grad_hidden)
    gate_up_grad = jnp.concatenate([grad_gate.astype(BF), grad_upward.astype(BF)], axis=1)
    grad_normed_two = scatter_rows(gate_up_grad, gate_up_weight, against)
    unused, second_pull = jax.vjp(rms_norm, after_attention, second_gain)
    grad_after, second_gain_grad = second_pull(grad_normed_two)
    grad_after = grad_after + grad_result
    down_sum = rows_out(transposed(hidden, grad_branch))
    gate_up_sum = columns_out(transposed(normed_two, gate_up_grad))
    gate_sum = join_columns(gate_up_sum[:, :, :hidden_width], shards)
    up_sum = join_columns(gate_up_sum[:, :, hidden_width:], shards)

    grad_out = gather_rows(grad_after.astype(BF))
    grad_mixed = against(grad_out, out_weight).astype(BF).reshape(length, heads, HD)
    output_grad = transposed(mixed, grad_out)
    if aligned:
        output_sum = rows_out(output_grad)
    else:
        output_sum = lax.psum_scatter(
            lax.dynamic_update_slice_in_dim(
                jnp.zeros((width, width), BF), output_grad.astype(BF), own * hw, 0
            ),
            ALL,
            scatter_dimension=0,
            tiled=True,
        ).astype(F32)
    grad_probs = jnp.einsum("qhd,khd->hqk", grad_mixed, value, preferred_element_type=F32)
    inner = jnp.sum(probs * grad_probs, axis=-1, keepdims=True)
    grad_scores = (probs * (grad_probs - inner)).astype(BF)
    grad_query = (
        jnp.einsum("hqk,khd->qhd", grad_scores, key, preferred_element_type=F32) * scale
    ).astype(BF)
    grad_key = (
        jnp.einsum("hqk,qhd->khd", grad_scores, query, preferred_element_type=F32) * scale
    ).astype(BF)
    grad_value = jnp.einsum("hqk,qhd->khd", weights, grad_mixed, preferred_element_type=F32)

    def rotated_back(values):
        return rotate(values.astype(F32), cosine, -sine).astype(BF).reshape(length, hw)

    qkv_grad = jnp.concatenate(
        [
            rotated_back(grad_query),
            rotated_back(grad_key),
            grad_value.astype(BF).reshape(length, hw),
        ],
        axis=1,
    )
    qkv_sum = columns_out(transposed(normed, qkv_grad))
    query_sum, key_sum, value_sum = (
        join_columns(qkv_sum[:, :, i * hw : (i + 1) * hw], head_blocks) for i in range(3)
    )
    grad_normed = scatter_rows(qkv_grad, qkv_weight, against)
    unused, first_pull = jax.vjp(rms_norm, inputs, first_gain)
    grad_inputs, first_gain_grad = first_pull(grad_normed)
    grad_inputs = grad_inputs + grad_after
    devices = shards * groups
    sums = sum_to_owners(
        jnp.concatenate(
            [
                first_gain_grad.reshape(devices, weight_rows),
                second_gain_grad.reshape(devices, weight_rows),
                jnp.full((devices, 128), error_sum),
            ],
            axis=1,
        )
    )
    output_shape = (sequences, local_rows, width)
    return (
        result.reshape(output_shape).astype(BF),
        sums[2 * weight_rows] / count,
        grad_inputs.reshape(output_shape),
        query_sum,
        key_sum,
        value_sum,
        output_sum,
        sums[:weight_rows],
        gate_sum,
        up_sum,
        down_sum,
        sums[weight_rows : 2 * weight_rows],
    )


def solution(mesh):
    rows = P("fsdp", "seq", None)
    places = P("fsdp", "seq")
    matrix = P(ALL, None)
    vector = P(ALL)
    return jax.shard_map(
        body,
        mesh=mesh,
        in_specs=(
            rows,
            rows,
            places,
            places,
            matrix,
            matrix,
            matrix,
            matrix,
            vector,
            matrix,
            matrix,
            matrix,
            vector,
        ),
        out_specs=(
            rows,
            P(),
            rows,
            matrix,
            matrix,
            matrix,
            matrix,
            vector,
            matrix,
            matrix,
            matrix,
            vector,
        ),
        check_vma=False,
    )
```

```python
import jax
import jax.numpy as jnp
from jax import lax
from jax.experimental import pallas as pl
from jax.experimental.pallas import tpu as pltpu
from jax.sharding import PartitionSpec as P

H = 32
HD = 64
EPSILON = 1e-05
ROPE_BASE = 130000.0
MASKED = -1e30
BF = jnp.bfloat16
F32 = jnp.float32
ALL = ("fsdp", "seq")


def rms_norm(values, gain_vector):
    return (
        values
        * lax.rsqrt(jnp.mean(values * values, axis=-1, keepdims=True) + EPSILON)
        * gain_vector
    )


def rope_tables(length):
    exponents = jnp.arange(HD // 2).astype(F32) * (2.0 / HD)
    inverse = jnp.power(ROPE_BASE, -exponents)
    angles = inverse[:, None] * jnp.arange(length, dtype=jnp.int32).astype(F32)[None, :]
    return jnp.cos(angles), jnp.sin(angles)


def matmul(left_side, right_side):
    return jnp.dot(left_side, right_side, preferred_element_type=F32)


def transposed(left_side, right_side):
    return lax.dot_general(
        left_side, right_side, (((0,), (0,)), ((), ())), preferred_element_type=F32
    )


def against(left_side, right_side):
    return lax.dot_general(
        left_side, right_side, (((1,), (1,)), ((), ())), preferred_element_type=F32
    )


def gated(gate_value, up_value):
    return gate_value * jax.nn.sigmoid(gate_value) * up_value


def turn(value, steps):
    size = lax.axis_size("seq")
    return lax.ppermute(value, "seq", [(s, (s - 2 * steps) % size) for s in range(size)])


def swap(value):
    return lax.ppermute(value, "seq", [(s, s ^ 1) for s in range(lax.axis_size("seq"))])


def beside(value, bit):
    return lax.ppermute(value, "fsdp", [(f, f ^ bit) for f in range(lax.axis_size("fsdp"))])


def place():
    own = lax.axis_index("seq")
    return own // 2, own % 2, lax.axis_size("seq") // 2


def tie(value, *others):
    anywhere = pl.BlockSpec(memory_space=pl.ANY)
    return pl.pallas_call(
        lambda *refs: None,
        out_shape=jax.ShapeDtypeStruct(value.shape, value.dtype),
        in_specs=[anywhere] * (1 + len(others)),
        out_specs=anywhere,
        input_output_aliases={0: 0},
        cost_estimate=pl.CostEstimate(flops=0, bytes_accessed=0, transcendentals=0),
    )(value, *others)


def order(chips):
    near = []
    for step in range(1, chips // 2 + 1):
        near += [step] if 2 * step == chips else [step, chips - step]
    return near


def gather_rows(local):
    return lax.all_gather(local, "seq", axis=0, tiled=True)


def scatter_rows(partial):
    return lax.psum_scatter(
        partial.astype(BF), "seq", scatter_dimension=0, tiled=True
    ).astype(F32)


def move(kernel, out_shapes, *operands, first=()):
    given = len(operands)
    whole = pl.BlockSpec(memory_space=pltpu.VMEM)
    many = isinstance(out_shapes, tuple)
    moved = sum(x.size * x.dtype.itemsize for x in operands)
    return pl.pallas_call(
        lambda *refs: kernel(*refs[:given], *refs[given + len(first) :]),
        out_shape=out_shapes,
        in_specs=[
            pl.BlockSpec(memory_space=pltpu.SMEM if x.ndim == 1 else pltpu.VMEM)
            for x in operands
        ]
        + [pl.BlockSpec(memory_space=pl.ANY)] * len(first),
        out_specs=tuple([whole] * len(out_shapes)) if many else whole,
        compiler_params=pltpu.CompilerParams(vmem_limit_bytes=48 * 2**20),
        cost_estimate=pl.CostEstimate(flops=0, bytes_accessed=3 * moved, transcendentals=0),
    )(*operands, *first)


def here():
    chip, core, chips = place()
    return jnp.stack([chip, core]).astype(jnp.int32)


def columns_of(weights, blocks, rows_of_extra=()):
    chip, core, chips = place()
    rows = weights[0].shape[0]
    parts = [w.shape[1] // (blocks * 2 * chips) for w in weights]
    cols = blocks * sum(parts) + (128 if rows_of_extra else 0)

    def kernel(at, *refs):
        out = refs[-1]
        chip, core = at[0], at[1]
        extra = []
        if rows_of_extra:
            filled = jnp.zeros((rows, 128), F32)
            which = lax.broadcasted_iota(jnp.int32, (rows, 128), 0)
            for i, ref in enumerate(refs[len(parts) : -1]):
                filled = jnp.where(which == i, ref[...], filled)
            extra = [filled.astype(BF)]
        for z in range(chips):
            for c in range(2):
                runs = []
                for ref, part in zip(refs, parts):
                    for b in range(blocks):
                        start = ((b * chips + z) * 2 + c) * part
                        runs.append(ref[:, start : start + part])
                out[(c + core) % 2, (z - chip + chips) % chips] = jnp.concatenate(
                    runs + extra, axis=1
                )

    return move(
        kernel,
        jax.ShapeDtypeStruct((2, chips, rows, cols), weights[0].dtype),
        here(),
        *weights,
        *rows_of_extra,
    )


def exchange(pieces, first=()):
    chip, core, chips = place()
    other = swap(pieces[1])
    shares = [jnp.stack([pieces[0, step], other[step]]) for step in range(chips)]
    if first:
        shares = [tie(share, *first) for share in shares]
    arrived = {0: shares[0]}
    for step in order(chips):
        arrived[chips - step] = turn(shares[step], -step)
    return [arrived[step] for step in range(chips)]


def rows_of(arrived, first=()):
    chip, core, chips = place()
    pair, rows, cols = arrived[0].shape

    def kernel(at, *refs):
        chip, core = at[0], at[1]
        for step in range(chips):
            for k in range(2):
                refs[-1][(chip + step) % chips, (core + k) % 2] = refs[step][k]

    return move(
        kernel,
        jax.ShapeDtypeStruct((chips, 2, rows, cols), arrived[0].dtype),
        here(),
        *arrived,
        first=first,
    ).reshape(chips * 2 * rows, cols)


def rows_to(summed):
    chip, core, chips = place()
    cols = summed.shape[1]
    rows = summed.shape[0] // (2 * chips)

    def kernel(at, ref, out):
        chip, core = at[0], at[1]
        for step in range(chips):
            for k in range(2):
                out[k, step] = ref[(chip + step) % chips, (core + k) % 2]

    return move(
        kernel,
        jax.ShapeDtypeStruct((2, chips, rows, cols), summed.dtype),
        here(),
        summed.reshape(chips, 2, rows, cols),
    )


def columns_to(arrived, blocks, widths):
    chip, core, chips = place()
    pair, rows, cols = arrived[0].shape
    parts = [w // blocks for w in widths]

    def kernel(at, *refs):
        chip, core = at[0], at[1]
        outs = refs[chips:]
        for step in range(chips):
            z = (chip + step) % chips
            at_col = 0
            for out, part in zip(outs, parts):
                for b in range(blocks):
                    one = refs[step][0, :, at_col : at_col + part].astype(F32)
                    two = refs[step][1, :, at_col : at_col + part].astype(F32)
                    both = jnp.concatenate(
                        [jnp.where(core == 0, one, two), jnp.where(core == 0, two, one)], axis=1
                    )
                    start = pl.multiple_of((b * chips + z) * 2 * part, 2 * part)
                    out[:, pl.ds(start, 2 * part)] = both
                    at_col += part

    return move(
        kernel,
        tuple(jax.ShapeDtypeStruct((rows, 2 * chips * w), F32) for w in widths),
        here(),
        *arrived,
    )


def square():
    return lax.axis_size("fsdp") == 4


def flipped(blocks):
    own = lax.axis_index("fsdp")
    odd, high = own % 2 == 1, own // 2 == 1
    a, b, c, d = blocks
    a, b, c, d = (
        jnp.where(odd, b, a),
        jnp.where(odd, a, b),
        jnp.where(odd, d, c),
        jnp.where(odd, c, d),
    )
    return [
        jnp.where(high, c, a),
        jnp.where(high, d, b),
        jnp.where(high, a, c),
        jnp.where(high, b, d),
    ]


def relative_blocks(values):
    if not square():
        return values
    return jnp.concatenate(flipped(jnp.split(values, 4, axis=-1)), axis=-1)


def gather_square(local, ordered=False):
    if not square():
        return lax.all_gather(local, "fsdp", axis=0, tiled=True), ((), ())
    half = local.shape[0] // 2
    one = beside(local, 1)
    two = beside(local, 2)
    three = beside(two[:half], 1)
    four = beside(one[half:], 2)
    steps = ((one, two), (three, four))
    if ordered:
        last = jnp.concatenate([three, four], axis=0)
        return jnp.concatenate(flipped([local, one, two, last]), axis=0), steps
    return jnp.concatenate([local, one, two, three, four], axis=0), steps


def begin_square(grad, ordered=False):
    grad = grad.astype(BF)
    if not square():
        return (lax.psum_scatter(grad, "fsdp", scatter_dimension=0, tiled=True),)
    rows, cols = grad.shape
    g = grad.reshape(4, 2, rows // 8, cols)
    if ordered:
        own = lax.axis_index("fsdp")
        g = [lax.dynamic_index_in_dim(g, own ^ i, 0, keepdims=False) for i in range(4)]
        g = {(i, j): g[i][j] for i in range(4) for j in range(2)}
    return (
        g,
        beside(jnp.stack([g[1, 0], g[3, 0]]), 1),
        beside(jnp.stack([g[2, 1], g[3, 1]]), 2),
    )


def second_square(g, one=None, two=None):
    if one is None:
        return (g,)
    def kernel(a, b, c, d, first, second):
        first[...] = (a[...].astype(F32) + b[1].astype(F32)).astype(BF)
        second[...] = (c[...].astype(F32) + d[1].astype(F32)).astype(BF)

    part = jax.ShapeDtypeStruct(g[2, 0].shape, BF)
    first, second = move(kernel, (part, part), g[2, 0], one, g[1, 1], two)
    return g, one, two, beside(first, 2), beside(second, 1)


def finish_square(g, one=None, two=None, one_last=None, two_last=None):
    if one is None:
        return g
    return jnp.concatenate(
        [
            g[0, 0].astype(F32) + one[0].astype(F32) + one_last.astype(F32),
            g[0, 1].astype(F32) + two[0].astype(F32) + two_last.astype(F32),
        ],
        axis=0,
    ).astype(BF)


def turned(values, cosine, sine):
    half = values.shape[0] // 2
    lead, trail = values[:half], values[half:]
    return jnp.concatenate([lead * cosine - trail * sine, trail * cosine + lead * sine], axis=0)


def dot(left_side, right_side):
    return jnp.dot(left_side, right_side, preferred_element_type=F32)


def seen_bias(column_ref, row_ref, bias_ref, block):
    length = row_ref.shape[1]
    for first in range(0, length, block):
        keys = first + block
        ahead = lax.broadcasted_iota(jnp.int32, (keys, block), 0) <= (
            lax.broadcasted_iota(jnp.int32, (keys, block), 1) + first
        )
        same = column_ref[:keys] == row_ref[:, first:keys]
        bias_ref[:keys, first:keys] = jnp.where(same & ahead, 0.0, MASKED)


def attend(qkv, cosine, sine, segment, block, heads):
    length = qkv.shape[1]
    scale = HD ** (-0.5)

    def kernel(q_ref, k_ref, v_ref, cos_ref, sin_ref, column_ref, row_ref, *refs):
        mixed_ref, query_ref, key_ref, value_ref, log_ref, bias_ref = refs

        @pl.when(pl.program_id(0) == 0)
        def _():
            seen_bias(column_ref, row_ref, bias_ref, block)

        cos, sin = cos_ref[...], sin_ref[...]
        query = turned(q_ref[...], cos, sin).astype(BF) * scale
        key_t = turned(k_ref[...], cos, sin).astype(BF)
        value_t = v_ref[...].astype(BF)
        query_ref[...] = query
        key_ref[...] = key_t
        value_ref[...] = value_t
        key = key_t.T
        for first in range(0, length, block):
            keys = first + block
            scores = dot(key[:keys], query[:, first:keys]) + bias_ref[:keys, first:keys]
            top = jnp.max(scores, axis=0, keepdims=True)
            exponent = jnp.exp(scores - top)
            total = jnp.sum(exponent, axis=0, keepdims=True)
            weights = (exponent * (1.0 / total)).astype(BF)
            mixed_ref[:, first:keys] = dot(value_t[:, :keys], weights).astype(BF)
            log_ref[0, :, first:keys] = top + jnp.log(total)

    head = lambda offset: pl.BlockSpec((HD, length), lambda h: (h + offset, 0))
    whole = pl.BlockSpec(memory_space=pltpu.VMEM)
    tall = jax.ShapeDtypeStruct((heads * HD, length), BF)
    return pl.pallas_call(
        kernel,
        grid=(heads,),
        out_shape=(tall, tall, tall, tall, jax.ShapeDtypeStruct((heads, 1, length), F32)),
        in_specs=[
            head(0),
            head(heads),
            head(2 * heads),
            whole,
            whole,
            whole,
            whole,
        ],
        out_specs=(
            head(0),
            head(0),
            head(0),
            head(0),
            pl.BlockSpec((1, 1, length), lambda h: (h, 0, 0)),
        ),
        scratch_shapes=[pltpu.VMEM((length, length), F32)],
        compiler_params=pltpu.CompilerParams(vmem_limit_bytes=56 * 2**20),
        cost_estimate=pl.CostEstimate(
            flops=4 * heads * HD * length * length,
            bytes_accessed=24 * heads * HD * length,
            transcendentals=heads * length * length,
        ),
    )(qkv, qkv, qkv, cosine, sine, segment[:, None], segment[None, :])


def attend_back(grad, query, key, value, logs, cosine, sine, segment, block, heads):
    length = grad.shape[1]
    scale = HD ** (-0.5)

    def kernel(grad_ref, query_ref, key_ref, value_ref, log_ref, *refs):
        cos_ref, sin_ref, column_ref, row_ref, dq_ref, dk_ref, dv_ref, bias_ref = refs[:8]
        key_sum, value_sum = refs[8:]

        @pl.when(pl.program_id(0) == 0)
        def _():
            seen_bias(column_ref, row_ref, bias_ref, block)

        cos, sin = cos_ref[...], sin_ref[...]
        grad_t = grad_ref[...]
        query_t, key_t = query_ref[...], key_ref[...]
        grads, queries, key, value = grad_t.T, query_t.T, key_t.T, value_ref[...].T
        for first in reversed(range(0, length, block)):
            keys = first + block
            here_q = slice(first, keys)
            scores = dot(key[:keys], query_t[:, here_q]) + bias_ref[:keys, here_q]
            probs = jnp.exp(scores - log_ref[0, :, here_q])
            grad_probs = dot(value[:keys], grad_t[:, here_q])
            inner = jnp.sum(probs * grad_probs, axis=0, keepdims=True)
            grad_scores = (probs * (grad_probs - inner)).astype(BF)
            key_part = dot(grad_scores, queries[here_q])
            value_part = dot(probs.astype(BF), grads[here_q])
            if keys == length:
                key_sum[...] = key_part
                value_sum[...] = value_part
            else:
                key_sum[:keys] += key_part
                value_sum[:keys] += value_part
            dq = (dot(key_t[:, :keys], grad_scores) * scale).astype(BF).astype(F32)
            dq_ref[:, here_q] = turned(dq, cos[:, here_q], -sin[:, here_q]).astype(BF)
        dk = key_sum[...].astype(BF).astype(F32).T
        dk_ref[...] = turned(dk, cos, -sin).astype(BF)
        dv_ref[...] = value_sum[...].T.astype(BF)

    head = pl.BlockSpec((HD, length), lambda h: (h, 0))
    whole = pl.BlockSpec(memory_space=pltpu.VMEM)
    tall = jax.ShapeDtypeStruct((heads * HD, length), BF)
    return pl.pallas_call(
        kernel,
        grid=(heads,),
        out_shape=(tall, tall, tall),
        in_specs=[
            head,
            head,
            head,
            head,
            pl.BlockSpec((1, 1, length), lambda h: (h, 0, 0)),
            whole,
            whole,
            whole,
            whole,
        ],
        out_specs=(head, head, head),
        scratch_shapes=[
            pltpu.VMEM((length, length), F32),
            pltpu.VMEM((length, HD), F32),
            pltpu.VMEM((length, HD), F32),
        ],
        compiler_params=pltpu.CompilerParams(vmem_limit_bytes=56 * 2**20),
        cost_estimate=pl.CostEstimate(
            flops=10 * heads * HD * length * length,
            bytes_accessed=24 * heads * HD * length,
            transcendentals=heads * length * length,
        ),
    )(grad, query, key, value, logs, cosine, sine, segment[:, None], segment[None, :])


def sum_to_owners(values):
    for axis in ALL:
        size, own = lax.axis_size(axis), lax.axis_index(axis)
        bit = size // 2
        while bit:
            halves = values.reshape(2, values.shape[0] // 2, values.shape[1])
            mine = (own // bit) % 2
            keep = lax.dynamic_index_in_dim(halves, mine, 0, keepdims=False)
            give = lax.dynamic_index_in_dim(halves, 1 - mine, 0, keepdims=False)
            values = keep + lax.ppermute(give, axis, [(s, s ^ bit) for s in range(size)])
            bit //= 2
    return values[0]


def body(
    tokens,
    teacher,
    segments,
    valid,
    query_weight,
    key_weight,
    value_weight,
    output_weight,
    attention_gain,
    gate_weight,
    up_weight,
    down_weight,
    mlp_gain,
):
    sequences, local_rows, width = tokens.shape
    groups = lax.axis_size("seq")
    shards = lax.axis_size("fsdp")
    heads = H // groups
    length = local_rows * groups
    own = lax.axis_index("seq")
    chip, core, chips = place()
    weight_rows = query_weight.shape[0]
    aligned = H % (shards * groups) == 0
    head_blocks = shards if aligned else 1
    hw = heads * HD

    inputs = tokens.reshape(local_rows, width).astype(F32)
    keep_mask = valid.reshape(local_rows).astype(F32)
    lane_pad = lambda row: jnp.pad(row, ((0, 0), (0, 128 - row.shape[1])))
    own_gains = jnp.concatenate([attention_gain, mlp_gain])[None, :]
    extra_rows = (
        lane_pad(own_gains.astype(F32)),
        lane_pad((segments // 256).astype(F32)),
        lane_pad((segments % 256).astype(F32)),
        jnp.broadcast_to(jnp.sum(keep_mask), (1, 128)),
    )
    attention_shares = exchange(
        columns_of([query_weight, key_weight, value_weight], head_blocks, extra_rows)
    )
    if aligned:
        out_weight, out_steps = gather_square(output_weight, ordered=True)
    else:
        out_weight = lax.dynamic_slice_in_dim(
            lax.all_gather(output_weight, ALL, axis=0, tiled=True), own * hw, hw, 0
        )
        out_steps = ((), ())
    down_full, down_steps = gather_square(down_weight, ordered=True)
    tokens_all = gather_rows(relative_blocks(tokens.reshape(local_rows, width)))
    attention_in, unused = gather_square(
        rows_of(attention_shares, first=down_steps[0])
    )
    gate_up_shares = exchange(
        columns_of([gate_weight, up_weight], shards), (attention_shares[chips // 2],)
    )
    gate_up_weight, gate_up_steps = gather_square(rows_of(gate_up_shares))

    qkv_weight = attention_in[:, : 3 * hw]
    extras = attention_in[:, 3 * hw :].reshape(shards * groups, weight_rows, 128).astype(F32)
    normed_gain = extras[:, 0, :weight_rows].reshape(width)
    gains = relative_blocks(
        jnp.stack([normed_gain, extras[:, 0, weight_rows : 2 * weight_rows].reshape(width)])
    )
    first_gain, second_gain = gains[0], gains[1]
    count = jnp.sum(extras[:, 3, 0])
    table = lax.dynamic_slice_in_dim(
        extras, 0 if square() else lax.axis_index("fsdp") * groups, groups, 0
    ).astype(jnp.int32)
    segment = (table[:, 1, :local_rows] * 256 + table[:, 2, :local_rows]).reshape(length)
    cosine, sine = rope_tables(length)

    normed = rms_norm(
        tokens_all.astype(F32), normed_gain
    ).astype(BF)
    qkv = lax.dot_general(
        qkv_weight, normed, (((0,), (1,)), ((), ())), preferred_element_type=F32
    )
    mixed, query, key, value, logs = attend(
        qkv, cosine, sine, segment, 2 * local_rows, heads
    )
    mixed = tie(mixed, *gate_up_shares[1:], *out_steps[1], *down_steps[1])
    after_attention = inputs + tie(
        scatter_rows(transposed(mixed, out_weight)), *gate_up_steps[0]
    )
    normed_two = gather_rows(
        relative_blocks(rms_norm(after_attention, second_gain).astype(BF))
    )
    gate_up = matmul(normed_two, gate_up_weight)
    hidden_width = gate_up.shape[1] // 2
    gate_value, up_value = gate_up[:, :hidden_width], gate_up[:, hidden_width:]
    hidden = gated(gate_value, up_value).astype(BF)
    result = after_attention + scatter_rows(matmul(hidden, down_full))
    difference = result - teacher.reshape(local_rows, width).astype(F32)
    error_sum = jnp.sum(keep_mask[:, None] * difference * difference)
    grad_result = 2.0 / count * keep_mask[:, None] * difference
    grad_branch = gather_rows(grad_result.astype(BF))
    unused, gate_pull = jax.vjp(gated, gate_value, up_value)
    grad_gate, grad_upward = gate_pull(against(grad_branch, down_full))
    gate_up_grad = jnp.concatenate([grad_gate.astype(BF), grad_upward.astype(BF)], axis=1)
    grad_normed_sum = against(gate_up_grad, gate_up_weight).astype(BF)
    grad_normed_two = scatter_rows(grad_normed_sum)
    gate_up_weight_grad = transposed(normed_two, tie(gate_up_grad, grad_normed_sum)).astype(BF)
    gate_up_back = begin_square(gate_up_weight_grad)
    down_grad = transposed(hidden, tie(grad_branch, gate_up_weight_grad)).astype(BF)
    grad_normed_two = relative_blocks(tie(grad_normed_two, down_grad))
    unused, second_pull = jax.vjp(rms_norm, after_attention, second_gain)
    grad_after, second_gain_grad = second_pull(grad_normed_two)
    grad_after = grad_after + grad_result

    grad_out = tie(gather_rows(grad_after.astype(BF)), *gate_up_back[1:])
    gate_up_back = second_square(*gate_up_back)
    grad_mixed = against(out_weight, grad_out).astype(BF)
    output_grad = matmul(mixed, grad_out)
    qkv_grad = jnp.concatenate(
        attend_back(
            grad_mixed, query, key, value, logs, cosine, sine, segment, 2 * local_rows, heads
        ),
        axis=0,
    )
    gate_up_back = finish_square(*gate_up_back[:-1], tie(gate_up_back[-1], qkv_grad))
    gate_up_shares = exchange(rows_to(gate_up_back))
    gate_sum, up_sum = columns_to(gate_up_shares, shards, [hidden_width, hidden_width])
    down_back = second_square(*begin_square(tie(down_grad, grad_mixed), ordered=True))
    down_sum = finish_square(*down_back).astype(F32)
    if aligned:
        output_back = second_square(*begin_square(output_grad, ordered=True))
        output_sum = finish_square(*output_back).astype(F32)
    else:
        output_sum = lax.psum_scatter(
            lax.dynamic_update_slice_in_dim(
                jnp.zeros((width, width), BF), output_grad.astype(BF), own * hw, 0
            ),
            ALL,
            scatter_dimension=0,
            tiled=True,
        ).astype(F32)
    qkv_back = begin_square(
        lax.dot_general(normed, qkv_grad, (((0,), (1,)), ((), ())), preferred_element_type=F32)
    )
    qkv_back = finish_square(*second_square(*qkv_back))
    query_sum, key_sum, value_sum = columns_to(
        exchange(rows_to(qkv_back)), head_blocks, [hw, hw, hw]
    )

    grad_normed = relative_blocks(
        scatter_rows(
            lax.dot_general(
                qkv_grad, qkv_weight, (((0,), (1,)), ((), ())), preferred_element_type=F32
            )
        )
    )
    unused, first_pull = jax.vjp(rms_norm, inputs, first_gain)
    grad_inputs, first_gain_grad = first_pull(grad_normed)
    grad_inputs = grad_inputs + grad_after
    devices = shards * groups
    sums = sum_to_owners(
        jnp.concatenate(
            [
                first_gain_grad.reshape(devices, weight_rows),
                second_gain_grad.reshape(devices, weight_rows),
                jnp.full((devices, 128), error_sum),
            ],
            axis=1,
        )
    )
    output_shape = (sequences, local_rows, width)
    return (
        result.reshape(output_shape).astype(BF),
        sums[2 * weight_rows] / count,
        grad_inputs.reshape(output_shape),
        query_sum,
        key_sum,
        value_sum,
        output_sum,
        sums[:weight_rows],
        gate_sum,
        up_sum,
        down_sum,
        sums[weight_rows : 2 * weight_rows],
    )


def solution(mesh):
    rows = P("fsdp", "seq", None)
    places = P("fsdp", "seq")
    matrix = P(ALL, None)
    vector = P(ALL)
    return jax.shard_map(
        body,
        mesh=mesh,
        in_specs=(
            rows,
            rows,
            places,
            places,
            matrix,
            matrix,
            matrix,
            matrix,
            vector,
            matrix,
            matrix,
            matrix,
            vector,
        ),
        out_specs=(
            rows,
            P(),
            rows,
            matrix,
            matrix,
            matrix,
            matrix,
            vector,
            matrix,
            matrix,
            matrix,
            vector,
        ),
        check_vma=False,
    )
```

```python
import jax
import jax.numpy as jnp
from jax import lax
from jax.experimental import pallas as pl
from jax.experimental.pallas import tpu as pltpu
from jax.sharding import PartitionSpec as P

H = 32
HD = 64
EPSILON = 1e-05
ROPE_BASE = 130000.0
MASKED = -1e30
BF = jnp.bfloat16
F32 = jnp.float32
ALL = ("fsdp", "seq")


def rms_norm(values, gain_vector):
    return (
        values
        * lax.rsqrt(jnp.mean(values * values, axis=-1, keepdims=True) + EPSILON)
        * gain_vector
    )


def rope_tables(length):
    exponents = jnp.arange(HD // 2).astype(F32) * (2.0 / HD)
    inverse = jnp.power(ROPE_BASE, -exponents)
    angles = inverse[:, None] * jnp.arange(length, dtype=jnp.int32).astype(F32)[None, :]
    return jnp.cos(angles), jnp.sin(angles)


def matmul(left_side, right_side):
    return jnp.dot(left_side, right_side, preferred_element_type=F32)


def transposed(left_side, right_side):
    return lax.dot_general(
        left_side, right_side, (((0,), (0,)), ((), ())), preferred_element_type=F32
    )


def against(left_side, right_side):
    return lax.dot_general(
        left_side, right_side, (((1,), (1,)), ((), ())), preferred_element_type=F32
    )


def gated(gate_value, up_value):
    return gate_value * jax.nn.sigmoid(gate_value) * up_value


def turn(value, steps):
    size = lax.axis_size("seq")
    return lax.ppermute(value, "seq", [(s, (s - 2 * steps) % size) for s in range(size)])


def swap(value):
    return lax.ppermute(value, "seq", [(s, s ^ 1) for s in range(lax.axis_size("seq"))])


def beside(value, bit):
    return lax.ppermute(value, "fsdp", [(f, f ^ bit) for f in range(lax.axis_size("fsdp"))])


def place():
    own = lax.axis_index("seq")
    return own // 2, own % 2, lax.axis_size("seq") // 2


def tie(value, *others):
    if not others:
        return value
    anywhere = pl.BlockSpec(memory_space=pl.ANY)
    return pl.pallas_call(
        lambda *refs: None,
        out_shape=jax.ShapeDtypeStruct(value.shape, value.dtype),
        in_specs=[anywhere] * (1 + len(others)),
        out_specs=anywhere,
        input_output_aliases={0: 0},
        cost_estimate=pl.CostEstimate(flops=0, bytes_accessed=0, transcendentals=0),
    )(value, *others)


def order(chips):
    near = []
    for step in range(1, chips // 2 + 1):
        near += [step] if 2 * step == chips else [step, chips - step]
    return near


def gather_rows(local):
    return lax.all_gather(local, "seq", axis=0, tiled=True)


def scatter_rows(partial):
    return lax.psum_scatter(partial, "seq", scatter_dimension=0, tiled=True)


def move(kernel, out_shapes, *operands, first=()):
    given = len(operands)
    whole = pl.BlockSpec(memory_space=pltpu.VMEM)
    many = isinstance(out_shapes, tuple)
    moved = sum(x.size * x.dtype.itemsize for x in operands)
    return pl.pallas_call(
        lambda *refs: kernel(*refs[:given], *refs[given + len(first) :]),
        out_shape=out_shapes,
        in_specs=[
            pl.BlockSpec(memory_space=pltpu.SMEM if x.ndim == 1 else pltpu.VMEM)
            for x in operands
        ]
        + [pl.BlockSpec(memory_space=pl.ANY)] * len(first),
        out_specs=tuple([whole] * len(out_shapes)) if many else whole,
        compiler_params=pltpu.CompilerParams(vmem_limit_bytes=48 * 2**20),
        cost_estimate=pl.CostEstimate(flops=0, bytes_accessed=3 * moved, transcendentals=0),
    )(*operands, *first)


def here():
    chip, core, chips = place()
    return jnp.stack([chip, core]).astype(jnp.int32)


def columns_of(weights, blocks, rows_of_extra=()):
    chip, core, chips = place()
    rows = weights[0].shape[0]
    parts = [w.shape[1] // (blocks * 2 * chips) for w in weights]
    cols = blocks * sum(parts) + (128 if rows_of_extra else 0)

    def kernel(at, *refs):
        chip, core = at[0], at[1]
        extra = []
        if rows_of_extra:
            filled = jnp.zeros((rows, 128), F32)
            which = lax.broadcasted_iota(jnp.int32, (rows, 128), 0)
            for i, ref in enumerate(refs[len(parts) : -2]):
                filled = jnp.where(which == i, ref[...], filled)
            extra = [filled.astype(BF)]
        for z in range(chips):
            sides = []
            for c in range(2):
                runs = []
                for ref, part in zip(refs, parts):
                    for b in range(blocks):
                        start = ((b * chips + z) * 2 + c) * part
                        runs.append(ref[:, start : start + part])
                sides.append(jnp.concatenate(runs + extra, axis=1))
            step = (z - chip + chips) % chips
            refs[-2][step] = jnp.where(core == 0, sides[0], sides[1])
            refs[-1][step] = jnp.where(core == 0, sides[1], sides[0])

    side = jax.ShapeDtypeStruct((chips, rows, cols), weights[0].dtype)
    return move(
        kernel,
        (side, side),
        here(),
        *weights,
        *rows_of_extra,
    )


def pairs_of(mine, given, first=()):
    chips = mine.shape[0]

    def kernel(one, two, *outs):
        for step, out in enumerate(outs):
            out[0] = one[step]
            out[1] = two[step]

    pair = jax.ShapeDtypeStruct((2, *mine.shape[1:]), mine.dtype)
    return move(kernel, (pair,) * chips, mine, swap(given), first=first)


def exchange(shares):
    chips = len(shares)
    arrived = {0: shares[0]}
    for step in order(chips):
        arrived[chips - step] = turn(shares[step], -step)
    return [arrived[step] for step in range(chips)]


def rows_of(arrived, first=()):
    chip, core, chips = place()
    pair, rows, cols = arrived[0].shape

    def kernel(at, *refs):
        chip, core = at[0], at[1]
        for step in range(chips):
            for k in range(2):
                refs[-1][(chip + step) % chips, (core + k) % 2] = refs[step][k]

    return move(
        kernel,
        jax.ShapeDtypeStruct((chips, 2, rows, cols), arrived[0].dtype),
        here(),
        *arrived,
        first=first,
    ).reshape(chips * 2 * rows, cols)


def rows_to(summed):
    chip, core, chips = place()
    cols = summed.shape[1]
    rows = summed.shape[0] // (2 * chips)

    def kernel(at, ref, mine, given):
        chip, core = at[0], at[1]
        for step in range(chips):
            mine[step] = ref[(chip + step) % chips, core]
            given[step] = ref[(chip + step) % chips, 1 - core]

    side = jax.ShapeDtypeStruct((chips, rows, cols), summed.dtype)
    return move(
        kernel,
        (side, side),
        here(),
        summed.reshape(chips, 2, rows, cols),
    )


def columns_to(arrived, blocks, widths, first=()):
    chip, core, chips = place()
    pair, rows, cols = arrived[0].shape
    parts = [w // blocks for w in widths]

    def kernel(at, *refs):
        chip, core = at[0], at[1]
        outs = refs[chips:]
        for step in range(chips):
            z = (chip + step) % chips
            at_col = 0
            for out, part in zip(outs, parts):
                for b in range(blocks):
                    one = refs[step][0, :, at_col : at_col + part].astype(F32)
                    two = refs[step][1, :, at_col : at_col + part].astype(F32)
                    both = jnp.concatenate(
                        [jnp.where(core == 0, one, two), jnp.where(core == 0, two, one)], axis=1
                    )
                    start = pl.multiple_of((b * chips + z) * 2 * part, 2 * part)
                    out[:, pl.ds(start, 2 * part)] = both
                    at_col += part

    return move(
        kernel,
        tuple(jax.ShapeDtypeStruct((rows, 2 * chips * w), F32) for w in widths),
        here(),
        *arrived,
        first=first,
    )


def square():
    return lax.axis_size("fsdp") == 4


def flipped(blocks):
    own = lax.axis_index("fsdp")
    odd, high = own % 2 == 1, own // 2 == 1
    a, b, c, d = blocks
    a, b, c, d = (
        jnp.where(odd, b, a),
        jnp.where(odd, a, b),
        jnp.where(odd, d, c),
        jnp.where(odd, c, d),
    )
    return [
        jnp.where(high, c, a),
        jnp.where(high, d, b),
        jnp.where(high, a, c),
        jnp.where(high, b, d),
    ]


def relative_blocks(values):
    if not square():
        return values
    return jnp.concatenate(flipped(jnp.split(values, 4, axis=-1)), axis=-1)


def gather_square(local, ordered=False, first=()):
    if not square():
        return lax.all_gather(local, "fsdp", axis=0, tiled=True), ((), ())
    rows, cols = local.shape
    half = rows // 2
    one = beside(local, 1)
    two = beside(local, 2)
    three = beside(two[:half], 1)
    four = beside(one[half:], 2)

    flip = lax.axis_index("fsdp") if ordered else jnp.int32(0)

    def kernel(at, *refs):
        for i, ref in enumerate(refs[:3]):
            refs[-1][i ^ at[0]] = ref[...]
        refs[-1][3 ^ at[0], :half] = refs[3][...]
        refs[-1][3 ^ at[0], half:] = refs[4][...]

    whole = move(
        kernel,
        jax.ShapeDtypeStruct((4, rows, cols), local.dtype),
        flip.astype(jnp.int32)[None],
        local,
        one,
        two,
        three,
        four,
        first=first,
    )
    return whole.reshape(4 * rows, cols), ((one, two), (three, four))


def weight_terms(rows, grads, blocks, out_rows, turned=(False, False), first=()):
    length = rows.shape[1 if turned[0] else 0]
    cols = grads.shape[0 if turned[1] else 1]

    def kernel(at, rows_ref, grads_ref, *refs):
        contract = (((1,), (1 if turned[1] else 0,)), ((), ()))
        left = rows_ref[...] if turned[0] else rows_ref[...].T
        refs[-1][0] = lax.dot_general(
            left, grads_ref[...], contract, preferred_element_type=F32
        ).astype(BF)

    return pl.pallas_call(
        kernel,
        grid_spec=pltpu.PrefetchScalarGridSpec(
            num_scalar_prefetch=1,
            grid=(blocks.shape[0],),
            in_specs=[
                pl.BlockSpec((out_rows, length), lambda i, at: (at[i], 0))
                if turned[0]
                else pl.BlockSpec((length, out_rows), lambda i, at: (0, at[i])),
                pl.BlockSpec(grads.shape, lambda i, at: (0, 0)),
            ]
            + [pl.BlockSpec(memory_space=pl.ANY)] * len(first),
            out_specs=pl.BlockSpec((1, out_rows, cols), lambda i, at: (i, 0, 0)),
        ),
        out_shape=jax.ShapeDtypeStruct((blocks.shape[0], out_rows, cols), BF),
        compiler_params=pltpu.CompilerParams(vmem_limit_bytes=48 * 2**20),
        cost_estimate=pl.CostEstimate(
            flops=2 * length * out_rows * cols * blocks.shape[0],
            bytes_accessed=2 * (length * (cols + out_rows * blocks.shape[0])),
            transcendentals=0,
        ),
    )(blocks, rows, grads, *first)


def begin_square(rows, grads, ordered=False, turned=(False, False), first=(), last=()):
    if not square():
        rows, grads = rows.T if turned[0] else rows, grads.T if turned[1] else grads
        terms = transposed(rows, grads).astype(BF)
        return (lax.psum_scatter(terms, "fsdp", scatter_dimension=0, tiled=True),), ()
    half = rows.shape[0 if turned[0] else 1] // 8
    flip = lax.axis_index("fsdp") if ordered else 0

    def terms(which, first):
        at = jnp.stack([2 * (jnp.int32(r) ^ flip) + h for r, h in which]).astype(jnp.int32)
        return weight_terms(rows, grads, at, half, turned, first)

    one = terms([(1, 0), (3, 0)], first)
    two = terms([(2, 1), (3, 1)], first)
    kept = terms([(2, 0), (1, 1), (0, 0), (0, 1)], (one, two, *last))
    return (kept, beside(one, 1), beside(two, 2)), (one, two)


def begin_square_of(terms, first=()):
    rows, cols = terms.shape
    half = rows // 8

    def kernel(at, g, one, two, kept):
        f = at[0]
        one[0], one[1] = g[1 ^ f, 0], g[3 ^ f, 0]
        two[0], two[1] = g[2 ^ f, 1], g[3 ^ f, 1]
        kept[0], kept[1] = g[2 ^ f, 0], g[1 ^ f, 1]
        kept[2], kept[3] = g[0 ^ f, 0], g[0 ^ f, 1]

    pair = jax.ShapeDtypeStruct((2, half, cols), BF)
    one, two, kept = move(
        kernel,
        (pair, pair, jax.ShapeDtypeStruct((4, half, cols), BF)),
        flip(),
        terms.reshape(4, 2, half, cols),
        first=first,
    )
    return kept, beside(one, 1), beside(two, 2)


def second_square(kept, one=None, two=None, first=()):
    if one is None:
        return (kept,)
    before = first

    def kernel(kept, one, two, first, second):
        first[...] = (kept[0].astype(F32) + one[1].astype(F32)).astype(BF)
        second[...] = (kept[1].astype(F32) + two[1].astype(F32)).astype(BF)

    part = jax.ShapeDtypeStruct(kept.shape[1:], BF)
    first, second = move(kernel, (part, part), kept, one, two, first=before)
    return kept, one, two, beside(first, 2), beside(second, 1)


def finish_square(
    kept, one=None, two=None, one_last=None, two_last=None, kind=BF, first=()
):
    if one is None:
        return kept.astype(kind)

    def kernel(kept, one, two, one_last, two_last, out):
        wide = lambda x: x.astype(F32)
        out[0] = (wide(kept[2]) + wide(one[0]) + wide(one_last[...])).astype(kind)
        out[1] = (wide(kept[3]) + wide(two[0]) + wide(two_last[...])).astype(kind)

    half, cols = kept.shape[1:]
    return move(
        kernel,
        jax.ShapeDtypeStruct((2, half, cols), kind),
        kept,
        one,
        two,
        one_last,
        two_last,
        first=first,
    ).reshape(2 * half, cols)


def turned(values, cosine, sine):
    half = values.shape[0] // 2
    lead, trail = values[:half], values[half:]
    return jnp.concatenate([lead * cosine - trail * sine, trail * cosine + lead * sine], axis=0)


def dot(left_side, right_side):
    return jnp.dot(left_side, right_side, preferred_element_type=F32)


def seen_bias(column_ref, row_ref, bias_ref, block):
    length = row_ref.shape[1]
    for first in range(0, length, block):
        keys = first + block
        ahead = lax.broadcasted_iota(jnp.int32, (keys, block), 0) <= (
            lax.broadcasted_iota(jnp.int32, (keys, block), 1) + first
        )
        same = column_ref[:keys] == row_ref[:, first:keys]
        bias_ref[:keys, first:keys] = jnp.where(same & ahead, 0.0, MASKED)


def attend(qkv, cosine, sine, segment, block, heads, first=()):
    length = qkv.shape[1]
    scale = HD ** (-0.5)

    def kernel(q_ref, k_ref, v_ref, cos_ref, sin_ref, column_ref, row_ref, *refs):
        mixed_ref, query_ref, key_ref, value_ref, log_ref, bias_ref = refs

        @pl.when(pl.program_id(0) == 0)
        def _():
            seen_bias(column_ref, row_ref, bias_ref, block)

        cos, sin = cos_ref[...], sin_ref[...]
        query = turned(q_ref[...], cos, sin).astype(BF) * scale
        key_t = turned(k_ref[...], cos, sin).astype(BF)
        value_t = v_ref[...].astype(BF)
        query_ref[...] = query
        key_ref[...] = key_t
        value_ref[...] = value_t
        key = key_t.T
        for first in range(0, length, block):
            keys = first + block
            scores = dot(key[:keys], query[:, first:keys]) + bias_ref[:keys, first:keys]
            top = jnp.max(scores, axis=0, keepdims=True)
            exponent = jnp.exp(scores - top)
            total = jnp.sum(exponent, axis=0, keepdims=True)
            weights = (exponent * (1.0 / total)).astype(BF)
            mixed_ref[:, first:keys] = dot(value_t[:, :keys], weights).astype(BF)
            log_ref[0, :, first:keys] = top + jnp.log(total)

    head = lambda offset: pl.BlockSpec((HD, length), lambda h: (h + offset, 0))
    whole = pl.BlockSpec(memory_space=pltpu.VMEM)
    tall = jax.ShapeDtypeStruct((heads * HD, length), BF)
    anywhere = pl.BlockSpec(memory_space=pl.ANY)
    return pl.pallas_call(
        lambda *refs: kernel(*refs[:7], *refs[7 + len(first) :]),
        grid=(heads,),
        out_shape=(tall, tall, tall, tall, jax.ShapeDtypeStruct((heads, 1, length), F32)),
        in_specs=[head(0), head(heads), head(2 * heads)]
        + [whole] * 4
        + [anywhere] * len(first),
        out_specs=(
            head(0),
            head(0),
            head(0),
            head(0),
            pl.BlockSpec((1, 1, length), lambda h: (h, 0, 0)),
        ),
        scratch_shapes=[pltpu.VMEM((length, length), F32)],
        compiler_params=pltpu.CompilerParams(vmem_limit_bytes=56 * 2**20),
        cost_estimate=pl.CostEstimate(
            flops=4 * heads * HD * length * length,
            bytes_accessed=24 * heads * HD * length,
            transcendentals=heads * length * length,
        ),
    )(qkv, qkv, qkv, cosine, sine, segment[:, None], segment[None, :], *first)


def attend_back(
    grad, query, key, value, logs, cosine, sine, segment, block, heads, first=()
):
    length = grad.shape[1]
    scale = HD ** (-0.5)

    def kernel(grad_ref, query_ref, key_ref, value_ref, log_ref, *refs):
        cos_ref, sin_ref, column_ref, row_ref, out_ref, bias_ref, key_sum, value_sum = refs

        @pl.when(pl.program_id(0) == 0)
        def _():
            seen_bias(column_ref, row_ref, bias_ref, block)

        cos, sin = cos_ref[...], sin_ref[...]
        grad_t = grad_ref[...]
        query_t, key_t = query_ref[...], key_ref[...]
        grads, queries, key, value = grad_t.T, query_t.T, key_t.T, value_ref[...].T
        for first in reversed(range(0, length, block)):
            keys = first + block
            here_q = slice(first, keys)
            scores = dot(key[:keys], query_t[:, here_q]) + bias_ref[:keys, here_q]
            probs = jnp.exp(scores - log_ref[0, :, here_q])
            grad_probs = dot(value[:keys], grad_t[:, here_q])
            inner = jnp.sum(probs * grad_probs, axis=0, keepdims=True)
            grad_scores = (probs * (grad_probs - inner)).astype(BF)
            key_part = dot(grad_scores, queries[here_q])
            value_part = dot(probs.astype(BF), grads[here_q])
            if keys == length:
                key_sum[...] = key_part
                value_sum[...] = value_part
            else:
                key_sum[:keys] += key_part
                value_sum[:keys] += value_part
            dq = (dot(key_t[:, :keys], grad_scores) * scale).astype(BF).astype(F32)
            out_ref[0, :, here_q] = turned(dq, cos[:, here_q], -sin[:, here_q]).astype(BF)
        dk = key_sum[...].astype(BF).astype(F32).T
        out_ref[1] = turned(dk, cos, -sin).astype(BF)
        out_ref[2] = value_sum[...].T.astype(BF)

    head = pl.BlockSpec((HD, length), lambda h: (h, 0))
    whole = pl.BlockSpec(memory_space=pltpu.VMEM)
    tall = jax.ShapeDtypeStruct((3, heads * HD, length), BF)
    return pl.pallas_call(
        lambda *refs: kernel(*refs[:9], *refs[9 + len(first) :]),
        grid=(heads,),
        out_shape=tall,
        in_specs=[
            head,
            head,
            head,
            head,
            pl.BlockSpec((1, 1, length), lambda h: (h, 0, 0)),
            whole,
            whole,
            whole,
            whole,
        ]
        + [pl.BlockSpec(memory_space=pl.ANY)] * len(first),
        out_specs=pl.BlockSpec((3, HD, length), lambda h: (0, h, 0)),
        scratch_shapes=[
            pltpu.VMEM((length, length), F32),
            pltpu.VMEM((length, HD), F32),
            pltpu.VMEM((length, HD), F32),
        ],
        compiler_params=pltpu.CompilerParams(vmem_limit_bytes=56 * 2**20),
        cost_estimate=pl.CostEstimate(
            flops=10 * heads * HD * length * length,
            bytes_accessed=24 * heads * HD * length,
            transcendentals=heads * length * length,
        ),
    )(grad, query, key, value, logs, cosine, sine, segment[:, None], segment[None, :], *first)


def gain_terms(grads, rows, scales, first=()):
    length, width = rows.shape
    block = 256

    def kernel(grad_ref, row_ref, scale_ref, *refs):
        total = jnp.zeros((1, block), F32)
        step = 256
        for at in range(0, length, step):
            terms = grad_ref[at : at + step].astype(F32) * row_ref[at : at + step].astype(F32)
            total += jnp.sum(terms * scale_ref[at : at + step], axis=0, keepdims=True)
        refs[-1][...] = total

    column = pl.BlockSpec((length, block), lambda i: (0, i))
    return pl.pallas_call(
        kernel,
        grid=(width // block,),
        out_shape=jax.ShapeDtypeStruct((1, width), F32),
        in_specs=[
            column,
            column,
            pl.BlockSpec((length, 1), lambda i: (0, 0)),
        ]
        + [pl.BlockSpec(memory_space=pl.ANY)] * len(first),
        out_specs=pl.BlockSpec((1, block), lambda i: (0, i)),
        cost_estimate=pl.CostEstimate(
            flops=4 * length * width, bytes_accessed=4 * length * width, transcendentals=0
        ),
    )(grads, rows, scales, *first).reshape(width)


def mlp(rows, gate_up_weight, down_full):
    length, width = rows.shape
    hidden_width = down_full.shape[0]
    tall, block = min(1024, length), min(256, hidden_width)
    steps = hidden_width // block

    def kernel(x_ref, gate_w, up_w, down_w, gate_ref, up_ref, hidden_ref, out_ref, total):
        x = x_ref[...]
        gate, up = dot(x, gate_w[...]), dot(x, up_w[...])
        hidden = gated(gate, up).astype(BF)
        gate_ref[...], up_ref[...], hidden_ref[...] = gate, up, hidden
        terms = dot(hidden, down_w[...])
        step = pl.program_id(1)

        @pl.when(step == 0)
        def _():
            total[...] = terms

        @pl.when((step > 0) & (step < steps - 1))
        def _():
            total[...] += terms

        @pl.when(step == steps - 1)
        def _():
            out_ref[...] = (total[...] + terms).astype(BF)

    part = pl.BlockSpec((tall, block), lambda i, j: (i, j))
    whole = pl.BlockSpec((tall, width), lambda i, j: (i, 0))
    wide = jax.ShapeDtypeStruct((length, hidden_width), F32)
    return pl.pallas_call(
        kernel,
        grid=(length // tall, steps),
        out_shape=(
            wide,
            wide,
            jax.ShapeDtypeStruct((length, hidden_width), BF),
            jax.ShapeDtypeStruct((length, width), BF),
        ),
        in_specs=[
            whole,
            pl.BlockSpec((width, block), lambda i, j: (0, j)),
            pl.BlockSpec((width, block), lambda i, j: (0, j + steps)),
            pl.BlockSpec((block, width), lambda i, j: (j, 0)),
        ],
        out_specs=(part, part, part, whole),
        scratch_shapes=[pltpu.VMEM((tall, width), F32)],
        compiler_params=pltpu.CompilerParams(vmem_limit_bytes=60 * 2**20),
        cost_estimate=pl.CostEstimate(
            flops=6 * length * width * hidden_width,
            bytes_accessed=6 * width * hidden_width + 4 * length * (width + 3 * hidden_width),
            transcendentals=length * hidden_width,
        ),
    )(rows, gate_up_weight, gate_up_weight, down_full)


def rows_back(columns, weight, first=()):
    inner, length = columns.shape
    width = weight.shape[0]
    block = 512

    def kernel(columns_ref, weight_ref, *refs):
        out_ref, rows_ref = refs[-2:]

        @pl.when(pl.program_id(0) == 0)
        def _():
            rows_ref[...] = columns_ref[...].T

        out_ref[...] = against(rows_ref[...], weight_ref[...]).astype(BF)

    return pl.pallas_call(
        kernel,
        grid=(width // block,),
        out_shape=jax.ShapeDtypeStruct((length, width), BF),
        in_specs=[
            pl.BlockSpec((inner, length), lambda j: (0, 0)),
            pl.BlockSpec((block, inner), lambda j: (j, 0)),
        ]
        + [pl.BlockSpec(memory_space=pl.ANY)] * len(first),
        out_specs=pl.BlockSpec((length, block), lambda j: (0, j)),
        scratch_shapes=[pltpu.VMEM((length, inner), BF)],
        compiler_params=pltpu.CompilerParams(vmem_limit_bytes=48 * 2**20),
        cost_estimate=pl.CostEstimate(
            flops=2 * length * width * inner,
            bytes_accessed=2 * (length * (width + inner) + width * inner),
            transcendentals=0,
        ),
    )(columns, weight, *first)


def flip():
    return (lax.axis_index("fsdp") if square() else jnp.int32(0)).astype(jnp.int32)[None]


def spots(at, width):
    size = width // 4
    return [pl.ds(pl.multiple_of((g ^ at[0]) * size, size), size) for g in range(4)]


def steadied(values):
    return lax.rsqrt(jnp.mean(values * values, axis=-1, keepdims=True) + EPSILON)


def after_first_sum(summed, tokens, gain, first):
    rows, width = tokens.shape

    def kernel(at, summed_ref, tokens_ref, gain_ref, attended_ref, normed_ref):
        values = tokens_ref[...].astype(F32) + summed_ref[...].astype(F32)
        attended_ref[...] = values
        normed = (values * steadied(values) * gain_ref[...]).astype(BF)
        for g, spot in enumerate(spots(at, width)):
            normed_ref[:, spot] = normed[:, g * (width // 4) : (g + 1) * (width // 4)]

    return move(
        kernel,
        (
            jax.ShapeDtypeStruct((rows, width), F32),
            jax.ShapeDtypeStruct((rows, width), BF),
        ),
        flip(),
        summed,
        tokens,
        gain[None, :],
        first=first,
    )


def after_second_sum(summed, attended, teacher, mask, weight):
    rows, width = attended.shape

    def kernel(summed_ref, attended_ref, teacher_ref, mask_ref, weight_ref, *outs):
        out_ref, grad_ref, low_ref, error_ref = outs
        result = attended_ref[...] + summed_ref[...].astype(F32)
        difference = result - teacher_ref[...].astype(F32)
        out_ref[...] = result.astype(BF)
        grad = weight_ref[...] * difference
        grad_ref[...] = grad
        low_ref[...] = grad.astype(BF)
        terms = jnp.sum(mask_ref[...] * difference * difference, axis=0, keepdims=True)
        error_ref[...] = jnp.broadcast_to(jnp.sum(terms, axis=1, keepdims=True), (1, 128))

    narrow = jax.ShapeDtypeStruct((rows, width), BF)
    wide = jax.ShapeDtypeStruct((rows, width), F32)
    return move(
        kernel,
        (narrow, wide, narrow, jax.ShapeDtypeStruct((1, 128), F32)),
        summed,
        attended,
        teacher,
        mask,
        weight,
    )


def after_third_sum(summed, attended, gain, grad_result, first):
    rows, width = attended.shape

    def kernel(at, summed_ref, attended_ref, gain_ref, result_ref, wide_ref, low_ref, gain_out):
        grads = jnp.concatenate([summed_ref[:, spot] for spot in spots(at, width)], axis=1)
        grads = grads.astype(F32)
        values = attended_ref[...]
        steady = steadied(values)
        gain_out[...] = jnp.sum(grads * values * steady, axis=0, keepdims=True)
        scaled = grads * gain_ref[...]
        inner = jnp.mean(scaled * values, axis=-1, keepdims=True)
        total = result_ref[...] + steady * scaled - values * (steady * steady * steady * inner)
        wide_ref[...] = total
        low_ref[...] = total.astype(BF)

    return move(
        kernel,
        (
            jax.ShapeDtypeStruct((rows, width), F32),
            jax.ShapeDtypeStruct((rows, width), BF),
            jax.ShapeDtypeStruct((1, width), F32),
        ),
        flip(),
        summed,
        attended,
        gain[None, :],
        grad_result,
        first=first,
    )


def after_last_sum(summed, tokens, gain, grad_after):
    rows, width = tokens.shape

    def kernel(at, summed_ref, tokens_ref, gain_ref, after_ref, out_ref):
        grads = jnp.concatenate([summed_ref[:, spot] for spot in spots(at, width)], axis=1)
        values = tokens_ref[...].astype(F32)
        steady = steadied(values)
        scaled = grads.astype(F32) * gain_ref[...]
        inner = jnp.mean(scaled * values, axis=-1, keepdims=True)
        out_ref[...] = (
            after_ref[...] + steady * scaled - values * (steady * steady * steady * inner)
        )

    return move(
        kernel,
        jax.ShapeDtypeStruct((rows, width), F32),
        flip(),
        summed,
        tokens,
        gain[None, :],
        grad_after,
    )


def sum_over_chips(values):
    chip, core, chips = place()
    shards, width = lax.axis_size("fsdp"), values.shape[1]
    own = lax.axis_index("fsdp")

    def share(values, at):
        return lax.dynamic_index_in_dim(values, at, 0, keepdims=False)

    values = values.reshape(shards, chips, 2, width)
    total = share(values, own)
    for step in range(1, shards):
        total += lax.ppermute(
            share(values, (own + step) % shards),
            "fsdp",
            [(f, (f + step) % shards) for f in range(shards)],
        )
    total = jnp.moveaxis(total, 1, 0)
    return share(total, core) + swap(share(total, 1 - core))


def sum_to_owners(values, first):
    chip, core, chips = place()
    values = tie(values, *first)

    def share(step):
        return lax.dynamic_index_in_dim(values, (chip + step) % chips, 0, keepdims=False)

    total = share(0)
    for step in order(chips):
        total += turn(share(step), -step)
    return total


def body(
    tokens,
    teacher,
    segments,
    valid,
    query_weight,
    key_weight,
    value_weight,
    output_weight,
    attention_gain,
    gate_weight,
    up_weight,
    down_weight,
    mlp_gain,
):
    sequences, local_rows, width = tokens.shape
    groups = lax.axis_size("seq")
    shards = lax.axis_size("fsdp")
    heads = H // groups
    length = local_rows * groups
    own = lax.axis_index("seq")
    chip, core, chips = place()
    weight_rows = query_weight.shape[0]
    aligned = H % (shards * groups) == 0
    head_blocks = shards if aligned else 1
    hw = heads * HD

    own_tokens = tokens.reshape(local_rows, width)
    keep_mask = valid.reshape(local_rows).astype(F32)
    lane_pad = lambda row: jnp.pad(row, ((0, 0), (0, 128 - row.shape[1])))
    own_gains = jnp.concatenate([attention_gain, mlp_gain])[None, :]
    extra_rows = (
        lane_pad(own_gains.astype(F32)),
        lane_pad((segments // 256).astype(F32)),
        lane_pad((segments % 256).astype(F32)),
        jnp.broadcast_to(jnp.sum(keep_mask), (1, 128)),
    )
    attention_shares = exchange(
        pairs_of(
            *columns_of([query_weight, key_weight, value_weight], head_blocks, extra_rows)
        )
    )
    if aligned:
        out_weight = lax.all_gather(output_weight, "fsdp", axis=0, tiled=True)
    else:
        out_weight = lax.dynamic_slice_in_dim(
            lax.all_gather(output_weight, ALL, axis=0, tiled=True), own * hw, hw, 0
        )
    down_full, down_steps = gather_square(down_weight, ordered=True)
    tokens_all = gather_rows(
        tie(relative_blocks(own_tokens), *attention_shares[1:], out_weight, *down_steps[0])
    )
    gate_up_shares = exchange(
        pairs_of(*columns_of([gate_weight, up_weight], shards), first=attention_shares[1:])
    )
    attention_in = gather_square(rows_of(attention_shares))[0]
    gate_up_weight, gate_up_steps = gather_square(rows_of(gate_up_shares))

    qkv_weight = attention_in[:, : 3 * hw]
    extras = attention_in[:, 3 * hw :].reshape(shards * groups, weight_rows, 128).astype(F32)
    normed_gain = extras[:, 0, :weight_rows].reshape(width)
    gains = relative_blocks(
        jnp.stack([normed_gain, extras[:, 0, weight_rows : 2 * weight_rows].reshape(width)])
    )
    first_gain, second_gain = gains[0], gains[1]
    count = jnp.sum(extras[:, 3, 0])
    table = lax.dynamic_slice_in_dim(
        extras, 0 if square() else lax.axis_index("fsdp") * groups, groups, 0
    ).astype(jnp.int32)
    segment = (table[:, 1, :local_rows] * 256 + table[:, 2, :local_rows]).reshape(length)
    cosine, sine = rope_tables(length)

    wide_tokens = tokens_all.astype(F32)
    steady = lax.rsqrt(jnp.mean(wide_tokens * wide_tokens, axis=-1, keepdims=True) + EPSILON)
    normed = (wide_tokens * steady * normed_gain).astype(BF)
    qkv = lax.dot_general(
        qkv_weight, normed, (((0,), (1,)), ((), ())), preferred_element_type=F32
    )
    mixed, query, key, value, logs = attend(
        qkv, cosine, sine, segment, 2 * local_rows, heads, first=(gate_up_shares[-1],)
    )
    mixed = tie(mixed, *gate_up_shares[1:], *down_steps[1])
    after_attention, normed_two = after_first_sum(
        scatter_rows(transposed(mixed, out_weight).astype(BF)),
        own_tokens,
        second_gain,
        gate_up_steps[0],
    )
    normed_two = gather_rows(normed_two)
    gate_value, up_value, hidden, partial = mlp(normed_two, gate_up_weight, down_full)
    hidden_width = hidden.shape[1]
    output, grad_result, grad_branch, error_sum = after_second_sum(
        scatter_rows(partial),
        after_attention,
        teacher.reshape(local_rows, width),
        keep_mask[:, None],
        (2.0 / count * keep_mask)[:, None],
    )
    grad_branch = gather_rows(grad_branch)
    unused, gate_pull = jax.vjp(gated, gate_value, up_value)
    grad_gate, grad_upward = gate_pull(against(grad_branch, down_full))
    grad_gate, grad_upward = grad_gate.astype(BF), grad_upward.astype(BF)
    grad_normed_sum = against(
        jnp.concatenate([grad_gate, grad_upward], axis=1), gate_up_weight
    ).astype(BF)
    gate_back, unused = begin_square(normed_two, grad_gate, first=(grad_normed_sum,))
    up_back, unused = begin_square(
        normed_two, grad_upward, first=(gate_back[0],), last=gate_back[1:]
    )
    grad_after, grad_out, second_gain_grad = after_third_sum(
        scatter_rows(grad_normed_sum),
        after_attention,
        second_gain,
        grad_result,
        up_back,
    )
    gate_back = second_square(*gate_back)

    grad_out = gather_rows(grad_out)
    up_back = second_square(*up_back)
    down_back, down_sent = begin_square(
        hidden, grad_branch, ordered=True, first=(gate_back[0],), last=up_back[3:]
    )
    gate_up_pairs = pairs_of(
        *rows_to(
            jnp.concatenate(
                [
                    finish_square(*gate_back, first=down_sent),
                    finish_square(*up_back),
                ],
                axis=1,
            )
        )
    )
    gate_up_shares = exchange(gate_up_pairs)
    grad_mixed = against(out_weight, grad_out).astype(BF)
    qkv_grad = attend_back(
        grad_mixed,
        query,
        key,
        value,
        logs,
        cosine,
        sine,
        segment,
        2 * local_rows,
        heads,
        first=gate_up_pairs,
    ).reshape(3 * hw, length)
    down_back = second_square(*down_back, first=gate_up_pairs)
    grad_normed_sum = rows_back(
        qkv_grad, attention_in, (*gate_up_shares[1:], *down_back[3:])
    )
    qkv_begun, unused = begin_square(
        normed, qkv_grad, turned=(False, True), first=(grad_normed_sum,)
    )
    first_gain_grad = gain_terms(grad_normed_sum, tokens_all, steady, qkv_begun[:1])
    output_grad = matmul(mixed, grad_out).astype(BF)
    if aligned and square():
        output_begun = begin_square_of(output_grad, first=qkv_begun[:1])
        qkv_back = second_square(*qkv_begun, first=(*output_begun, first_gain_grad))
        output_back = second_square(*output_begun)
        output_sum = finish_square(*output_back, kind=F32)
    else:
        qkv_back = second_square(*qkv_begun, first=(first_gain_grad,))
        output_back = ()
        output_sum = lax.psum_scatter(
            lax.dynamic_update_slice_in_dim(
                jnp.zeros((width, width), BF), output_grad, own * hw, 0
            ),
            ALL,
            scatter_dimension=0,
            tiled=True,
        ).astype(F32)
    devices = shards * groups
    sums = sum_over_chips(
        jnp.concatenate(
            [
                relative_blocks(first_gain_grad).reshape(devices, weight_rows),
                second_gain_grad.reshape(devices, weight_rows),
                jnp.broadcast_to(error_sum, (devices, 128)),
            ],
            axis=1,
        )
    )
    qkv_pairs = pairs_of(
        *rows_to(finish_square(*qkv_back)), first=(sums, *output_back[3:])
    )
    qkv_shares = exchange(qkv_pairs)
    query_sum, key_sum, value_sum = columns_to(qkv_shares, head_blocks, [hw, hw, hw])
    gate_sum, up_sum = columns_to(
        gate_up_shares, shards, [hidden_width, hidden_width], first=qkv_pairs[:1]
    )
    down_sum = finish_square(*down_back, kind=F32, first=qkv_pairs[:1])
    grad_inputs = after_last_sum(
        scatter_rows(grad_normed_sum), own_tokens, first_gain, grad_after
    )
    sums = sum_to_owners(
        sums, (*qkv_shares[1:], gate_sum, down_sum, grad_inputs, output_sum)
    )
    output_shape = (sequences, local_rows, width)
    return (
        output.reshape(output_shape),
        sums[2 * weight_rows] / count,
        grad_inputs.reshape(output_shape),
        query_sum,
        key_sum,
        value_sum,
        output_sum,
        sums[:weight_rows],
        gate_sum,
        up_sum,
        down_sum,
        sums[weight_rows : 2 * weight_rows],
    )


def solution(mesh):
    rows = P("fsdp", "seq", None)
    places = P("fsdp", "seq")
    matrix = P(ALL, None)
    vector = P(ALL)
    return jax.shard_map(
        body,
        mesh=mesh,
        in_specs=(
            rows,
            rows,
            places,
            places,
            matrix,
            matrix,
            matrix,
            matrix,
            vector,
            matrix,
            matrix,
            matrix,
            vector,
        ),
        out_specs=(
            rows,
            P(),
            rows,
            matrix,
            matrix,
            matrix,
            matrix,
            vector,
            matrix,
            matrix,
            matrix,
            vector,
        ),
        check_vma=False,
    )
```

```python
import jax
import jax.numpy as jnp
from jax import lax
from jax.experimental import pallas as pl
from jax.experimental.pallas import tpu as pltpu
from jax.sharding import PartitionSpec as P

H = 32
HD = 64
EPSILON = 1e-05
ROPE_BASE = 130000.0
MASKED = -1e30
BF = jnp.bfloat16
F32 = jnp.float32
ALL = ("fsdp", "seq")


def rms_norm(values, gain_vector):
    return (
        values
        * lax.rsqrt(jnp.mean(values * values, axis=-1, keepdims=True) + EPSILON)
        * gain_vector
    )


def rope_tables(length):
    exponents = jnp.arange(HD // 2).astype(F32) * (2.0 / HD)
    inverse = jnp.power(ROPE_BASE, -exponents)
    angles = inverse[:, None] * jnp.arange(length, dtype=jnp.int32).astype(F32)[None, :]
    return jnp.cos(angles), jnp.sin(angles)


def matmul(left_side, right_side):
    return jnp.dot(left_side, right_side, preferred_element_type=F32)


def transposed(left_side, right_side):
    return lax.dot_general(
        left_side, right_side, (((0,), (0,)), ((), ())), preferred_element_type=F32
    )


def against(left_side, right_side):
    return lax.dot_general(
        left_side, right_side, (((1,), (1,)), ((), ())), preferred_element_type=F32
    )


def gated(gate_value, up_value):
    return gate_value * jax.nn.sigmoid(gate_value) * up_value


def turn(value, steps):
    size = lax.axis_size("seq")
    return lax.ppermute(value, "seq", [(s, (s - 2 * steps) % size) for s in range(size)])


def swap(value):
    return lax.ppermute(value, "seq", [(s, s ^ 1) for s in range(lax.axis_size("seq"))])


def beside(value, bit):
    return lax.ppermute(value, "fsdp", [(f, f ^ bit) for f in range(lax.axis_size("fsdp"))])


def place():
    own = lax.axis_index("seq")
    return own // 2, own % 2, lax.axis_size("seq") // 2


def tie(value, *others):
    if not others:
        return value
    anywhere = pl.BlockSpec(memory_space=pl.ANY)
    return pl.pallas_call(
        lambda *refs: None,
        out_shape=jax.ShapeDtypeStruct(value.shape, value.dtype),
        in_specs=[anywhere] * (1 + len(others)),
        out_specs=anywhere,
        input_output_aliases={0: 0},
        cost_estimate=pl.CostEstimate(flops=0, bytes_accessed=0, transcendentals=0),
    )(value, *others)


def order(chips):
    near = []
    for step in range(1, chips // 2 + 1):
        near += [step] if 2 * step == chips else [step, chips - step]
    return near


def gather_rows(local):
    return lax.all_gather(local, "seq", axis=0, tiled=True)


def scatter_rows(partial):
    return lax.psum_scatter(partial, "seq", scatter_dimension=0, tiled=True)


def move(kernel, out_shapes, *operands, first=()):
    given = len(operands)
    whole = pl.BlockSpec(memory_space=pltpu.VMEM)
    many = isinstance(out_shapes, tuple)
    moved = sum(x.size * x.dtype.itemsize for x in operands)
    return pl.pallas_call(
        lambda *refs: kernel(*refs[:given], *refs[given + len(first) :]),
        out_shape=out_shapes,
        in_specs=[
            pl.BlockSpec(memory_space=pltpu.SMEM if x.ndim == 1 else pltpu.VMEM)
            for x in operands
        ]
        + [pl.BlockSpec(memory_space=pl.ANY)] * len(first),
        out_specs=tuple([whole] * len(out_shapes)) if many else whole,
        compiler_params=pltpu.CompilerParams(vmem_limit_bytes=48 * 2**20),
        cost_estimate=pl.CostEstimate(flops=0, bytes_accessed=3 * moved, transcendentals=0),
    )(*operands, *first)


def here():
    chip, core, chips = place()
    return jnp.stack([chip, core]).astype(jnp.int32)


def columns_of(weights, blocks, rows_of_extra=()):
    chip, core, chips = place()
    rows = weights[0].shape[0]
    parts = [w.shape[1] // (blocks * 2 * chips) for w in weights]
    cols = blocks * sum(parts) + (128 if rows_of_extra else 0)

    def kernel(at, *refs):
        chip, core = at[0], at[1]
        extra = []
        if rows_of_extra:
            filled = jnp.zeros((rows, 128), F32)
            which = lax.broadcasted_iota(jnp.int32, (rows, 128), 0)
            for i, ref in enumerate(refs[len(parts) : -2]):
                filled = jnp.where(which == i, ref[...], filled)
            extra = [filled.astype(BF)]
        for z in range(chips):
            sides = []
            for c in range(2):
                runs = []
                for ref, part in zip(refs, parts):
                    for b in range(blocks):
                        start = ((b * chips + z) * 2 + c) * part
                        runs.append(ref[:, start : start + part])
                sides.append(jnp.concatenate(runs + extra, axis=1))
            step = (z - chip + chips) % chips
            refs[-2][step] = jnp.where(core == 0, sides[0], sides[1])
            refs[-1][step] = jnp.where(core == 0, sides[1], sides[0])

    side = jax.ShapeDtypeStruct((chips, rows, cols), weights[0].dtype)
    return move(
        kernel,
        (side, side),
        here(),
        *weights,
        *rows_of_extra,
    )


def pairs_of(mine, given, first=()):
    chips = mine.shape[0]

    def kernel(one, two, *outs):
        for step, out in enumerate(outs):
            out[0] = one[step]
            out[1] = two[step]

    pair = jax.ShapeDtypeStruct((2, *mine.shape[1:]), mine.dtype)
    return move(kernel, (pair,) * chips, mine, swap(given), first=first)


def exchange(shares):
    chips = len(shares)
    arrived = {0: shares[0]}
    for step in order(chips):
        arrived[chips - step] = turn(shares[step], -step)
    return [arrived[step] for step in range(chips)]


def rows_of(arrived, first=()):
    chip, core, chips = place()
    pair, rows, cols = arrived[0].shape

    def kernel(at, *refs):
        chip, core = at[0], at[1]
        for step in range(chips):
            for k in range(2):
                refs[-1][(chip + step) % chips, (core + k) % 2] = refs[step][k]

    return move(
        kernel,
        jax.ShapeDtypeStruct((chips, 2, rows, cols), arrived[0].dtype),
        here(),
        *arrived,
        first=first,
    ).reshape(chips * 2 * rows, cols)


def rows_to(summed):
    chip, core, chips = place()
    cols = summed.shape[1]
    rows = summed.shape[0] // (2 * chips)

    def kernel(at, ref, mine, given):
        chip, core = at[0], at[1]
        for step in range(chips):
            mine[step] = ref[(chip + step) % chips, core]
            given[step] = ref[(chip + step) % chips, 1 - core]

    side = jax.ShapeDtypeStruct((chips, rows, cols), summed.dtype)
    return move(
        kernel,
        (side, side),
        here(),
        summed.reshape(chips, 2, rows, cols),
    )


def columns_to(arrived, blocks, widths, first=()):
    chip, core, chips = place()
    pair, rows, cols = arrived[0].shape
    parts = [w // blocks for w in widths]

    def kernel(at, *refs):
        chip, core = at[0], at[1]
        outs = refs[chips:]
        for step in range(chips):
            z = (chip + step) % chips
            at_col = 0
            for out, part in zip(outs, parts):
                for b in range(blocks):
                    one = refs[step][0, :, at_col : at_col + part].astype(F32)
                    two = refs[step][1, :, at_col : at_col + part].astype(F32)
                    both = jnp.concatenate(
                        [jnp.where(core == 0, one, two), jnp.where(core == 0, two, one)], axis=1
                    )
                    start = pl.multiple_of((b * chips + z) * 2 * part, 2 * part)
                    out[:, pl.ds(start, 2 * part)] = both
                    at_col += part

    return move(
        kernel,
        tuple(jax.ShapeDtypeStruct((rows, 2 * chips * w), F32) for w in widths),
        here(),
        *arrived,
        first=first,
    )


def square():
    return lax.axis_size("fsdp") == 4


def flipped(blocks):
    own = lax.axis_index("fsdp")
    odd, high = own % 2 == 1, own // 2 == 1
    a, b, c, d = blocks
    a, b, c, d = (
        jnp.where(odd, b, a),
        jnp.where(odd, a, b),
        jnp.where(odd, d, c),
        jnp.where(odd, c, d),
    )
    return [
        jnp.where(high, c, a),
        jnp.where(high, d, b),
        jnp.where(high, a, c),
        jnp.where(high, b, d),
    ]


def relative_blocks(values):
    if not square():
        return values
    return jnp.concatenate(flipped(jnp.split(values, 4, axis=-1)), axis=-1)


def gather_square(local, ordered=False, first=()):
    if not square():
        return lax.all_gather(local, "fsdp", axis=0, tiled=True), ((), ())
    rows, cols = local.shape
    half = rows // 2
    one = beside(local, 1)
    two = beside(local, 2)
    three = beside(two[:half], 1)
    four = beside(one[half:], 2)

    flip = lax.axis_index("fsdp") if ordered else jnp.int32(0)

    def kernel(at, *refs):
        for i, ref in enumerate(refs[:3]):
            refs[-1][i ^ at[0]] = ref[...]
        refs[-1][3 ^ at[0], :half] = refs[3][...]
        refs[-1][3 ^ at[0], half:] = refs[4][...]

    whole = move(
        kernel,
        jax.ShapeDtypeStruct((4, rows, cols), local.dtype),
        flip.astype(jnp.int32)[None],
        local,
        one,
        two,
        three,
        four,
        first=first,
    )
    return whole.reshape(4 * rows, cols), ((one, two), (three, four))


def weight_terms(rows, grads, blocks, out_rows, turned=(False, False), first=()):
    length = rows.shape[1 if turned[0] else 0]
    cols = grads.shape[0 if turned[1] else 1]

    def kernel(at, rows_ref, grads_ref, *refs):
        contract = (((1,), (1 if turned[1] else 0,)), ((), ()))
        left = rows_ref[...] if turned[0] else rows_ref[...].T
        refs[-1][0] = lax.dot_general(
            left, grads_ref[...], contract, preferred_element_type=F32
        ).astype(BF)

    return pl.pallas_call(
        kernel,
        grid_spec=pltpu.PrefetchScalarGridSpec(
            num_scalar_prefetch=1,
            grid=(blocks.shape[0],),
            in_specs=[
                pl.BlockSpec((out_rows, length), lambda i, at: (at[i], 0))
                if turned[0]
                else pl.BlockSpec((length, out_rows), lambda i, at: (0, at[i])),
                pl.BlockSpec(grads.shape, lambda i, at: (0, 0)),
            ]
            + [pl.BlockSpec(memory_space=pl.ANY)] * len(first),
            out_specs=pl.BlockSpec((1, out_rows, cols), lambda i, at: (i, 0, 0)),
        ),
        out_shape=jax.ShapeDtypeStruct((blocks.shape[0], out_rows, cols), BF),
        compiler_params=pltpu.CompilerParams(vmem_limit_bytes=48 * 2**20),
        cost_estimate=pl.CostEstimate(
            flops=2 * length * out_rows * cols * blocks.shape[0],
            bytes_accessed=2 * (length * (cols + out_rows * blocks.shape[0])),
            transcendentals=0,
        ),
    )(blocks, rows, grads, *first)


def begin_square(rows, grads, ordered=False, turned=(False, False), first=()):
    if not square():
        rows, grads = rows.T if turned[0] else rows, grads.T if turned[1] else grads
        terms = transposed(rows, grads).astype(BF)
        summed = lax.psum_scatter(terms, "fsdp", scatter_dimension=0, tiled=True)
        return lambda *last: (summed,), ()
    half = rows.shape[0 if turned[0] else 1] // 8
    flip = lax.axis_index("fsdp") if ordered else 0

    def terms(which, first):
        at = jnp.stack([2 * (jnp.int32(r) ^ flip) + h for r, h in which]).astype(jnp.int32)
        return weight_terms(rows, grads, at, half, turned, first)

    one = terms([(1, 0), (3, 0)], first)
    two = terms([(2, 1), (3, 1)], first)

    def keep(*last):
        kept = terms([(2, 0), (1, 1), (0, 0), (0, 1)], (one, two, *last))
        return kept, beside(one, 1), beside(two, 2)

    return keep, (one, two)


def begin_square_of(terms, first=()):
    rows, cols = terms.shape
    half = rows // 8

    def kernel(at, g, one, two, kept):
        f = at[0]
        one[0], one[1] = g[1 ^ f, 0], g[3 ^ f, 0]
        two[0], two[1] = g[2 ^ f, 1], g[3 ^ f, 1]
        kept[0], kept[1] = g[2 ^ f, 0], g[1 ^ f, 1]
        kept[2], kept[3] = g[0 ^ f, 0], g[0 ^ f, 1]

    pair = jax.ShapeDtypeStruct((2, half, cols), BF)
    one, two, kept = move(
        kernel,
        (pair, pair, jax.ShapeDtypeStruct((4, half, cols), BF)),
        flip(),
        terms.reshape(4, 2, half, cols),
        first=first,
    )
    return kept, beside(one, 1), beside(two, 2)


def second_square(kept, one=None, two=None, first=()):
    if one is None:
        return (kept,)
    before = first

    def kernel(kept, one, two, first, second):
        first[...] = (kept[0].astype(F32) + one[1].astype(F32)).astype(BF)
        second[...] = (kept[1].astype(F32) + two[1].astype(F32)).astype(BF)

    part = jax.ShapeDtypeStruct(kept.shape[1:], BF)
    first, second = move(kernel, (part, part), kept, one, two, first=before)
    return kept, one, two, beside(first, 2), beside(second, 1)


def finish_square(
    kept, one=None, two=None, one_last=None, two_last=None, kind=BF, first=()
):
    if one is None:
        return kept.astype(kind)

    def kernel(kept, one, two, one_last, two_last, out):
        wide = lambda x: x.astype(F32)
        out[0] = (wide(kept[2]) + wide(one[0]) + wide(one_last[...])).astype(kind)
        out[1] = (wide(kept[3]) + wide(two[0]) + wide(two_last[...])).astype(kind)

    half, cols = kept.shape[1:]
    return move(
        kernel,
        jax.ShapeDtypeStruct((2, half, cols), kind),
        kept,
        one,
        two,
        one_last,
        two_last,
        first=first,
    ).reshape(2 * half, cols)


def turned(values, cosine, sine):
    half = values.shape[0] // 2
    lead, trail = values[:half], values[half:]
    return jnp.concatenate([lead * cosine - trail * sine, trail * cosine + lead * sine], axis=0)


def dot(left_side, right_side):
    return jnp.dot(left_side, right_side, preferred_element_type=F32)


def seen_bias(column_ref, row_ref, bias_ref, block):
    length = row_ref.shape[1]
    for first in range(0, length, block):
        keys = first + block
        ahead = lax.broadcasted_iota(jnp.int32, (keys, block), 0) <= (
            lax.broadcasted_iota(jnp.int32, (keys, block), 1) + first
        )
        same = column_ref[:keys] == row_ref[:, first:keys]
        bias_ref[:keys, first:keys] = jnp.where(same & ahead, 0.0, MASKED)


def attend(qkv, cosine, sine, segment, block, heads, first=()):
    length = qkv.shape[1]
    scale = HD ** (-0.5)

    def kernel(q_ref, k_ref, v_ref, cos_ref, sin_ref, column_ref, row_ref, *refs):
        mixed_ref, query_ref, key_ref, value_ref, log_ref, bias_ref = refs

        @pl.when(pl.program_id(0) == 0)
        def _():
            seen_bias(column_ref, row_ref, bias_ref, block)

        cos, sin = cos_ref[...], sin_ref[...]
        query = turned(q_ref[...], cos, sin).astype(BF) * scale
        key_t = turned(k_ref[...], cos, sin).astype(BF)
        value_t = v_ref[...].astype(BF)
        query_ref[...] = query
        key_ref[...] = key_t
        value_ref[...] = value_t
        key = key_t.T
        for first in range(0, length, block):
            keys = first + block
            scores = dot(key[:keys], query[:, first:keys]) + bias_ref[:keys, first:keys]
            top = jnp.max(scores, axis=0, keepdims=True)
            exponent = jnp.exp(scores - top)
            total = jnp.sum(exponent, axis=0, keepdims=True)
            weights = (exponent * (1.0 / total)).astype(BF)
            mixed_ref[:, first:keys] = dot(value_t[:, :keys], weights).astype(BF)
            log_ref[0, :, first:keys] = top + jnp.log(total)

    head = lambda offset: pl.BlockSpec((HD, length), lambda h: (h + offset, 0))
    whole = pl.BlockSpec(memory_space=pltpu.VMEM)
    tall = jax.ShapeDtypeStruct((heads * HD, length), BF)
    anywhere = pl.BlockSpec(memory_space=pl.ANY)
    return pl.pallas_call(
        lambda *refs: kernel(*refs[:7], *refs[7 + len(first) :]),
        grid=(heads,),
        out_shape=(tall, tall, tall, tall, jax.ShapeDtypeStruct((heads, 1, length), F32)),
        in_specs=[head(0), head(heads), head(2 * heads)]
        + [whole] * 4
        + [anywhere] * len(first),
        out_specs=(
            head(0),
            head(0),
            head(0),
            head(0),
            pl.BlockSpec((1, 1, length), lambda h: (h, 0, 0)),
        ),
        scratch_shapes=[pltpu.VMEM((length, length), F32)],
        compiler_params=pltpu.CompilerParams(vmem_limit_bytes=56 * 2**20),
        cost_estimate=pl.CostEstimate(
            flops=4 * heads * HD * length * length,
            bytes_accessed=24 * heads * HD * length,
            transcendentals=heads * length * length,
        ),
    )(qkv, qkv, qkv, cosine, sine, segment[:, None], segment[None, :], *first)


def attend_back(
    grad, query, key, value, logs, cosine, sine, segment, block, heads, first=()
):
    length = grad.shape[1]
    scale = HD ** (-0.5)

    def kernel(grad_ref, query_ref, key_ref, value_ref, log_ref, *refs):
        cos_ref, sin_ref, column_ref, row_ref, out_ref, bias_ref, key_sum, value_sum = refs

        @pl.when(pl.program_id(0) == 0)
        def _():
            seen_bias(column_ref, row_ref, bias_ref, block)

        cos, sin = cos_ref[...], sin_ref[...]
        grad_t = grad_ref[...]
        query_t, key_t = query_ref[...], key_ref[...]
        grads, queries, key, value = grad_t.T, query_t.T, key_t.T, value_ref[...].T
        for first in reversed(range(0, length, block)):
            keys = first + block
            here_q = slice(first, keys)
            scores = dot(key[:keys], query_t[:, here_q]) + bias_ref[:keys, here_q]
            probs = jnp.exp(scores - log_ref[0, :, here_q])
            grad_probs = dot(value[:keys], grad_t[:, here_q])
            inner = jnp.sum(probs * grad_probs, axis=0, keepdims=True)
            grad_scores = (probs * (grad_probs - inner)).astype(BF)
            key_part = dot(grad_scores, queries[here_q])
            value_part = dot(probs.astype(BF), grads[here_q])
            if keys == length:
                key_sum[...] = key_part
                value_sum[...] = value_part
            else:
                key_sum[:keys] += key_part
                value_sum[:keys] += value_part
            dq = (dot(key_t[:, :keys], grad_scores) * scale).astype(BF).astype(F32)
            out_ref[0, :, here_q] = turned(dq, cos[:, here_q], -sin[:, here_q]).astype(BF)
        dk = key_sum[...].astype(BF).astype(F32).T
        out_ref[1] = turned(dk, cos, -sin).astype(BF)
        out_ref[2] = value_sum[...].T.astype(BF)

    head = pl.BlockSpec((HD, length), lambda h: (h, 0))
    whole = pl.BlockSpec(memory_space=pltpu.VMEM)
    tall = jax.ShapeDtypeStruct((3, heads * HD, length), BF)
    return pl.pallas_call(
        lambda *refs: kernel(*refs[:9], *refs[9 + len(first) :]),
        grid=(heads,),
        out_shape=tall,
        in_specs=[
            head,
            head,
            head,
            head,
            pl.BlockSpec((1, 1, length), lambda h: (h, 0, 0)),
            whole,
            whole,
            whole,
            whole,
        ]
        + [pl.BlockSpec(memory_space=pl.ANY)] * len(first),
        out_specs=pl.BlockSpec((3, HD, length), lambda h: (0, h, 0)),
        scratch_shapes=[
            pltpu.VMEM((length, length), F32),
            pltpu.VMEM((length, HD), F32),
            pltpu.VMEM((length, HD), F32),
        ],
        compiler_params=pltpu.CompilerParams(vmem_limit_bytes=56 * 2**20),
        cost_estimate=pl.CostEstimate(
            flops=10 * heads * HD * length * length,
            bytes_accessed=24 * heads * HD * length,
            transcendentals=heads * length * length,
        ),
    )(grad, query, key, value, logs, cosine, sine, segment[:, None], segment[None, :], *first)


def gain_terms(grads, rows, scales, first=()):
    length, width = rows.shape
    block = 256

    def kernel(grad_ref, row_ref, scale_ref, *refs):
        total = jnp.zeros((1, block), F32)
        step = 256
        for at in range(0, length, step):
            terms = grad_ref[at : at + step].astype(F32) * row_ref[at : at + step].astype(F32)
            total += jnp.sum(terms * scale_ref[at : at + step], axis=0, keepdims=True)
        refs[-1][...] = total

    column = pl.BlockSpec((length, block), lambda i: (0, i))
    return pl.pallas_call(
        kernel,
        grid=(width // block,),
        out_shape=jax.ShapeDtypeStruct((1, width), F32),
        in_specs=[
            column,
            column,
            pl.BlockSpec((length, 1), lambda i: (0, 0)),
        ]
        + [pl.BlockSpec(memory_space=pl.ANY)] * len(first),
        out_specs=pl.BlockSpec((1, block), lambda i: (0, i)),
        cost_estimate=pl.CostEstimate(
            flops=4 * length * width, bytes_accessed=4 * length * width, transcendentals=0
        ),
    )(grads, rows, scales, *first).reshape(width)


def mlp(rows, gate_up_weight, down_full):
    length, width = rows.shape
    hidden_width = down_full.shape[0]
    tall, block, wide = min(1024, length), min(256, hidden_width), 512
    steps, ends = hidden_width // block, width // wide

    def kernel(x_ref, gate_w, up_w, down_w, gate_ref, up_ref, hidden_ref, out_ref, kept):
        step = pl.program_id(1)

        @pl.when(step < steps)
        def _():
            x = x_ref[...]
            gate, up = dot(x, gate_w[...]), dot(x, up_w[...])
            hidden = gated(gate, up).astype(BF)
            gate_ref[...], up_ref[...], hidden_ref[...] = gate, up, hidden
            kept[jnp.minimum(step, steps - 1)] = hidden

        @pl.when(step >= steps)
        def _():
            hidden = jnp.concatenate([kept[i] for i in range(steps)], axis=1)
            out_ref[...] = dot(hidden, down_w[...]).astype(BF)

    early = lambda j: jnp.minimum(j, steps - 1)
    late = lambda j: jnp.maximum(j - steps, 0)
    part = pl.BlockSpec((tall, block), lambda i, j: (i, early(j)))
    full = jax.ShapeDtypeStruct((length, hidden_width), F32)
    return pl.pallas_call(
        kernel,
        grid=(length // tall, steps + ends),
        out_shape=(
            full,
            full,
            jax.ShapeDtypeStruct((length, hidden_width), BF),
            jax.ShapeDtypeStruct((length, width), BF),
        ),
        in_specs=[
            pl.BlockSpec((tall, width), lambda i, j: (i, 0)),
            pl.BlockSpec((width, block), lambda i, j: (0, early(j))),
            pl.BlockSpec((width, block), lambda i, j: (0, early(j) + steps)),
            pl.BlockSpec((hidden_width, wide), lambda i, j: (0, late(j))),
        ],
        out_specs=(part, part, part, pl.BlockSpec((tall, wide), lambda i, j: (i, late(j)))),
        scratch_shapes=[pltpu.VMEM((steps, tall, block), BF)],
        compiler_params=pltpu.CompilerParams(vmem_limit_bytes=56 * 2**20),
        cost_estimate=pl.CostEstimate(
            flops=6 * length * width * hidden_width,
            bytes_accessed=6 * width * hidden_width + 4 * length * (width + 3 * hidden_width),
            transcendentals=length * hidden_width,
        ),
    )(rows, gate_up_weight, gate_up_weight, down_full)


def mlp_back(grads, gate, up, gate_up_weight, down_full):
    length, width = grads.shape
    hidden_width = down_full.shape[0]
    tall, block, wide = min(1024, length), min(256, hidden_width), 512
    steps, ends = hidden_width // block, width // wide

    def kernel(g_ref, gate_ref, up_ref, down_w, both_w, dgate, dup, out_ref, kept):
        step = pl.program_id(1)

        @pl.when(step < steps)
        def _():
            gate, up = gate_ref[...], up_ref[...]
            share = jax.nn.sigmoid(gate)
            grad_hidden = against(g_ref[...], down_w[...])
            grad_gate = (grad_hidden * up * (share + gate * share * (1.0 - share))).astype(BF)
            grad_up = (grad_hidden * (gate * share)).astype(BF)
            dgate[...], dup[...] = grad_gate, grad_up
            at = jnp.minimum(step, steps - 1)
            kept[at] = grad_gate
            kept[at + steps] = grad_up

        @pl.when(step >= steps)
        def _():
            both = jnp.concatenate([kept[i] for i in range(2 * steps)], axis=1)
            out_ref[...] = against(both, both_w[...]).astype(BF)

    early = lambda j: jnp.minimum(j, steps - 1)
    late = lambda j: jnp.maximum(j - steps, 0)
    part = pl.BlockSpec((tall, block), lambda i, j: (i, early(j)))
    narrow = jax.ShapeDtypeStruct((length, hidden_width), BF)
    return pl.pallas_call(
        kernel,
        grid=(length // tall, steps + ends),
        out_shape=(narrow, narrow, jax.ShapeDtypeStruct((length, width), BF)),
        in_specs=[
            pl.BlockSpec((tall, width), lambda i, j: (i, 0)),
            part,
            part,
            pl.BlockSpec((block, width), lambda i, j: (early(j), 0)),
            pl.BlockSpec((wide, 2 * hidden_width), lambda i, j: (late(j), 0)),
        ],
        out_specs=(part, part, pl.BlockSpec((tall, wide), lambda i, j: (i, late(j)))),
        scratch_shapes=[pltpu.VMEM((2 * steps, tall, block), BF)],
        compiler_params=pltpu.CompilerParams(vmem_limit_bytes=56 * 2**20),
        cost_estimate=pl.CostEstimate(
            flops=6 * length * width * hidden_width,
            bytes_accessed=6 * width * hidden_width + 4 * length * (width + 3 * hidden_width),
            transcendentals=length * hidden_width,
        ),
    )(grads, gate, up, down_full, gate_up_weight)


def rows_back(columns, weight, first=()):
    inner, length = columns.shape
    width = weight.shape[0]
    block = 512

    def kernel(columns_ref, weight_ref, *refs):
        out_ref, rows_ref = refs[-2:]

        @pl.when(pl.program_id(0) == 0)
        def _():
            rows_ref[...] = columns_ref[...].T

        out_ref[...] = against(rows_ref[...], weight_ref[...]).astype(BF)

    return pl.pallas_call(
        kernel,
        grid=(width // block,),
        out_shape=jax.ShapeDtypeStruct((length, width), BF),
        in_specs=[
            pl.BlockSpec((inner, length), lambda j: (0, 0)),
            pl.BlockSpec((block, inner), lambda j: (j, 0)),
        ]
        + [pl.BlockSpec(memory_space=pl.ANY)] * len(first),
        out_specs=pl.BlockSpec((length, block), lambda j: (0, j)),
        scratch_shapes=[pltpu.VMEM((length, inner), BF)],
        compiler_params=pltpu.CompilerParams(vmem_limit_bytes=48 * 2**20),
        cost_estimate=pl.CostEstimate(
            flops=2 * length * width * inner,
            bytes_accessed=2 * (length * (width + inner) + width * inner),
            transcendentals=0,
        ),
    )(columns, weight, *first)


def flip():
    return (lax.axis_index("fsdp") if square() else jnp.int32(0)).astype(jnp.int32)[None]


def spots(at, width):
    size = width // 4
    return [pl.ds(pl.multiple_of((g ^ at[0]) * size, size), size) for g in range(4)]


def steadied(values):
    return lax.rsqrt(jnp.mean(values * values, axis=-1, keepdims=True) + EPSILON)


def after_first_sum(summed, tokens, gain, first):
    rows, width = tokens.shape

    def kernel(at, summed_ref, tokens_ref, gain_ref, attended_ref, normed_ref):
        values = tokens_ref[...].astype(F32) + summed_ref[...].astype(F32)
        attended_ref[...] = values
        normed = (values * steadied(values) * gain_ref[...]).astype(BF)
        for g, spot in enumerate(spots(at, width)):
            normed_ref[:, spot] = normed[:, g * (width // 4) : (g + 1) * (width // 4)]

    return move(
        kernel,
        (
            jax.ShapeDtypeStruct((rows, width), F32),
            jax.ShapeDtypeStruct((rows, width), BF),
        ),
        flip(),
        summed,
        tokens,
        gain[None, :],
        first=first,
    )


def after_second_sum(summed, attended, teacher, mask, weight):
    rows, width = attended.shape

    def kernel(summed_ref, attended_ref, teacher_ref, mask_ref, weight_ref, *outs):
        out_ref, grad_ref, low_ref, error_ref = outs
        result = attended_ref[...] + summed_ref[...].astype(F32)
        difference = result - teacher_ref[...].astype(F32)
        out_ref[...] = result.astype(BF)
        grad = weight_ref[...] * difference
        grad_ref[...] = grad
        low_ref[...] = grad.astype(BF)
        terms = jnp.sum(mask_ref[...] * difference * difference, axis=0, keepdims=True)
        error_ref[...] = jnp.broadcast_to(jnp.sum(terms, axis=1, keepdims=True), (1, 128))

    narrow = jax.ShapeDtypeStruct((rows, width), BF)
    wide = jax.ShapeDtypeStruct((rows, width), F32)
    return move(
        kernel,
        (narrow, wide, narrow, jax.ShapeDtypeStruct((1, 128), F32)),
        summed,
        attended,
        teacher,
        mask,
        weight,
    )


def after_third_sum(summed, attended, gain, grad_result, first):
    rows, width = attended.shape

    def kernel(at, summed_ref, attended_ref, gain_ref, result_ref, wide_ref, low_ref, gain_out):
        grads = jnp.concatenate([summed_ref[:, spot] for spot in spots(at, width)], axis=1)
        grads = grads.astype(F32)
        values = attended_ref[...]
        steady = steadied(values)
        gain_out[...] = jnp.sum(grads * values * steady, axis=0, keepdims=True)
        scaled = grads * gain_ref[...]
        inner = jnp.mean(scaled * values, axis=-1, keepdims=True)
        total = result_ref[...] + steady * scaled - values * (steady * steady * steady * inner)
        wide_ref[...] = total
        low_ref[...] = total.astype(BF)

    return move(
        kernel,
        (
            jax.ShapeDtypeStruct((rows, width), F32),
            jax.ShapeDtypeStruct((rows, width), BF),
            jax.ShapeDtypeStruct((1, width), F32),
        ),
        flip(),
        summed,
        attended,
        gain[None, :],
        grad_result,
        first=first,
    )


def after_last_sum(summed, tokens, gain, grad_after):
    rows, width = tokens.shape

    def kernel(at, summed_ref, tokens_ref, gain_ref, after_ref, out_ref):
        grads = jnp.concatenate([summed_ref[:, spot] for spot in spots(at, width)], axis=1)
        values = tokens_ref[...].astype(F32)
        steady = steadied(values)
        scaled = grads.astype(F32) * gain_ref[...]
        inner = jnp.mean(scaled * values, axis=-1, keepdims=True)
        out_ref[...] = (
            after_ref[...] + steady * scaled - values * (steady * steady * steady * inner)
        )

    return move(
        kernel,
        jax.ShapeDtypeStruct((rows, width), F32),
        flip(),
        summed,
        tokens,
        gain[None, :],
        grad_after,
    )


def sum_to_owners(values):
    chip, core, chips = place()
    shards, width = lax.axis_size("fsdp"), values.shape[1]
    own = lax.axis_index("fsdp")

    def share(values, at):
        return lax.dynamic_index_in_dim(values, at, 0, keepdims=False)

    values = values.reshape(shards, chips, 2, width)
    total = share(values, own)
    for step in range(1, shards):
        total += lax.ppermute(
            share(values, (own + step) % shards),
            "fsdp",
            [(f, (f + step) % shards) for f in range(shards)],
        )
    total = jnp.moveaxis(total, 1, 0)
    values = share(total, core) + swap(share(total, 1 - core))
    total = share(values, chip)
    for step in order(chips):
        total += turn(share(values, (chip + step) % chips), -step)
    return total


def body(
    tokens,
    teacher,
    segments,
    valid,
    query_weight,
    key_weight,
    value_weight,
    output_weight,
    attention_gain,
    gate_weight,
    up_weight,
    down_weight,
    mlp_gain,
):
    sequences, local_rows, width = tokens.shape
    groups = lax.axis_size("seq")
    shards = lax.axis_size("fsdp")
    heads = H // groups
    length = local_rows * groups
    own = lax.axis_index("seq")
    chip, core, chips = place()
    weight_rows = query_weight.shape[0]
    aligned = H % (shards * groups) == 0
    head_blocks = shards if aligned else 1
    hw = heads * HD

    own_tokens = tokens.reshape(local_rows, width)
    keep_mask = valid.reshape(local_rows).astype(F32)
    lane_pad = lambda row: jnp.pad(row, ((0, 0), (0, 128 - row.shape[1])))
    own_gains = jnp.concatenate([attention_gain, mlp_gain])[None, :]
    extra_rows = (
        lane_pad(own_gains.astype(F32)),
        lane_pad((segments // 256).astype(F32)),
        lane_pad((segments % 256).astype(F32)),
        jnp.broadcast_to(jnp.sum(keep_mask), (1, 128)),
    )
    attention_shares = exchange(
        pairs_of(
            *columns_of([query_weight, key_weight, value_weight], head_blocks, extra_rows)
        )
    )
    if aligned:
        out_weight = lax.all_gather(output_weight, "fsdp", axis=0, tiled=True)
    else:
        out_weight = lax.dynamic_slice_in_dim(
            lax.all_gather(output_weight, ALL, axis=0, tiled=True), own * hw, hw, 0
        )
    down_full, down_steps = gather_square(down_weight, ordered=True)
    tokens_all = gather_rows(
        tie(relative_blocks(own_tokens), *attention_shares[1:], out_weight, *down_steps[0])
    )
    gate_up_shares = exchange(
        pairs_of(*columns_of([gate_weight, up_weight], shards), first=attention_shares[1:])
    )
    attention_in = gather_square(rows_of(attention_shares))[0]
    gate_up_weight, gate_up_steps = gather_square(rows_of(gate_up_shares))

    qkv_weight = attention_in[:, : 3 * hw]
    extras = attention_in[:, 3 * hw :].reshape(shards * groups, weight_rows, 128).astype(F32)
    normed_gain = extras[:, 0, :weight_rows].reshape(width)
    gains = relative_blocks(
        jnp.stack([normed_gain, extras[:, 0, weight_rows : 2 * weight_rows].reshape(width)])
    )
    first_gain, second_gain = gains[0], gains[1]
    count = jnp.sum(extras[:, 3, 0])
    table = lax.dynamic_slice_in_dim(
        extras, 0 if square() else lax.axis_index("fsdp") * groups, groups, 0
    ).astype(jnp.int32)
    segment = (table[:, 1, :local_rows] * 256 + table[:, 2, :local_rows]).reshape(length)
    cosine, sine = rope_tables(length)

    wide_tokens = tokens_all.astype(F32)
    steady = lax.rsqrt(jnp.mean(wide_tokens * wide_tokens, axis=-1, keepdims=True) + EPSILON)
    normed = (wide_tokens * steady * normed_gain).astype(BF)
    qkv = lax.dot_general(
        qkv_weight, normed, (((0,), (1,)), ((), ())), preferred_element_type=F32
    )
    mixed, query, key, value, logs = attend(
        qkv, cosine, sine, segment, 2 * local_rows, heads, first=(gate_up_shares[-1],)
    )
    mixed = tie(mixed, *gate_up_shares[1:], *down_steps[1])
    after_attention, normed_two = after_first_sum(
        scatter_rows(transposed(mixed, out_weight).astype(BF)),
        own_tokens,
        second_gain,
        gate_up_steps[0],
    )
    normed_two = gather_rows(normed_two)
    gate_value, up_value, hidden, partial = mlp(normed_two, gate_up_weight, down_full)
    hidden_width = hidden.shape[1]
    output, grad_result, grad_branch, error_sum = after_second_sum(
        scatter_rows(partial),
        after_attention,
        teacher.reshape(local_rows, width),
        keep_mask[:, None],
        (2.0 / count * keep_mask)[:, None],
    )
    grad_branch = gather_rows(grad_branch)
    grad_gate, grad_upward, grad_normed_sum = mlp_back(
        grad_branch, gate_value, up_value, gate_up_weight, down_full
    )
    gate_keep, unused = begin_square(normed_two, grad_gate, first=(grad_normed_sum,))
    gate_back = gate_keep()
    up_keep, unused = begin_square(normed_two, grad_upward, first=gate_back[:1])
    up_back = up_keep(*gate_back[1:])
    grad_after, grad_out, second_gain_grad = after_third_sum(
        scatter_rows(grad_normed_sum),
        after_attention,
        second_gain,
        grad_result,
        up_back,
    )
    gate_back = second_square(*gate_back)

    grad_out = gather_rows(grad_out)
    up_back = second_square(*up_back)
    down_keep, down_sent = begin_square(hidden, grad_branch, ordered=True, first=gate_back[:1])
    down_back = down_keep()
    gate_up_pairs = pairs_of(
        *rows_to(
            jnp.concatenate(
                [
                    finish_square(*gate_back, first=down_sent),
                    finish_square(*up_back, first=down_back[:1]),
                ],
                axis=1,
            )
        )
    )
    gate_up_shares = exchange(gate_up_pairs)
    grad_mixed = against(out_weight, grad_out).astype(BF)
    qkv_grad = attend_back(
        grad_mixed,
        query,
        key,
        value,
        logs,
        cosine,
        sine,
        segment,
        2 * local_rows,
        heads,
        first=gate_up_pairs,
    ).reshape(3 * hw, length)
    down_back = second_square(*down_back, first=gate_up_pairs)
    grad_normed_sum = rows_back(
        qkv_grad, attention_in, (*gate_up_shares[1:], *down_back[3:])
    )
    qkv_keep, qkv_sent = begin_square(
        normed, qkv_grad, turned=(False, True), first=(grad_normed_sum,)
    )
    first_gain_grad = gain_terms(grad_normed_sum, tokens_all, steady, qkv_sent)
    qkv_begun = qkv_keep(first_gain_grad)
    output_grad = matmul(mixed, grad_out).astype(BF)
    if aligned and square():
        output_begun = begin_square_of(output_grad, first=qkv_begun[:1])
        qkv_back = second_square(*qkv_begun, first=output_begun[:1])
        output_back = second_square(*output_begun)
        output_sum = finish_square(*output_back, kind=F32)
    else:
        qkv_back = second_square(*qkv_begun)
        output_begun = ()
        output_sum = lax.psum_scatter(
            lax.dynamic_update_slice_in_dim(
                jnp.zeros((width, width), BF), output_grad, own * hw, 0
            ),
            ALL,
            scatter_dimension=0,
            tiled=True,
        ).astype(F32)
    devices = shards * groups
    sums = sum_to_owners(
        jnp.concatenate(
            [
                relative_blocks(first_gain_grad).reshape(devices, weight_rows),
                second_gain_grad.reshape(devices, weight_rows),
                jnp.broadcast_to(error_sum, (devices, 128)),
            ],
            axis=1,
        )
    )
    qkv_pairs = pairs_of(
        *rows_to(finish_square(*qkv_back)), first=(sums, *output_begun[1:])
    )
    qkv_shares = exchange(qkv_pairs)
    gate_sum, up_sum = columns_to(
        gate_up_shares, shards, [hidden_width, hidden_width], first=qkv_back[3:4]
    )
    down_sum = finish_square(*down_back, kind=F32, first=qkv_back[3:4])
    grad_inputs = after_last_sum(
        scatter_rows(grad_normed_sum), own_tokens, first_gain, grad_after
    )
    query_sum, key_sum, value_sum = columns_to(
        qkv_shares,
        head_blocks,
        [hw, hw, hw],
        first=(gate_sum, down_sum, grad_inputs, output_sum),
    )
    output_shape = (sequences, local_rows, width)
    return (
        output.reshape(output_shape),
        sums[2 * weight_rows] / count,
        grad_inputs.reshape(output_shape),
        query_sum,
        key_sum,
        value_sum,
        output_sum,
        sums[:weight_rows],
        gate_sum,
        up_sum,
        down_sum,
        sums[weight_rows : 2 * weight_rows],
    )


def solution(mesh):
    rows = P("fsdp", "seq", None)
    places = P("fsdp", "seq")
    matrix = P(ALL, None)
    vector = P(ALL)
    return jax.shard_map(
        body,
        mesh=mesh,
        in_specs=(
            rows,
            rows,
            places,
            places,
            matrix,
            matrix,
            matrix,
            matrix,
            vector,
            matrix,
            matrix,
            matrix,
            vector,
        ),
        out_specs=(
            rows,
            P(),
            rows,
            matrix,
            matrix,
            matrix,
            matrix,
            vector,
            matrix,
            matrix,
            matrix,
            vector,
        ),
        check_vma=False,
    )
```

```python
import jax
import jax.numpy as jnp
from jax import lax
from jax.experimental import pallas as pl
from jax.experimental.pallas import tpu as pltpu
from jax.sharding import PartitionSpec as P

H = 32
HD = 64
EPSILON = 1e-05
ROPE_BASE = 130000.0
MASKED = -1e30
BF = jnp.bfloat16
F32 = jnp.float32
ALL = ("fsdp", "seq")


def rms_norm(values, gain_vector):
    return (
        values
        * lax.rsqrt(jnp.mean(values * values, axis=-1, keepdims=True) + EPSILON)
        * gain_vector
    )


def rope_tables(length):
    exponents = jnp.arange(HD // 2).astype(F32) * (2.0 / HD)
    inverse = jnp.power(ROPE_BASE, -exponents)
    angles = inverse[:, None] * jnp.arange(length, dtype=jnp.int32).astype(F32)[None, :]
    return jnp.cos(angles), jnp.sin(angles)


def matmul(left_side, right_side):
    return jnp.dot(left_side, right_side, preferred_element_type=F32)


def transposed(left_side, right_side):
    return lax.dot_general(
        left_side, right_side, (((0,), (0,)), ((), ())), preferred_element_type=F32
    )


def against(left_side, right_side):
    return lax.dot_general(
        left_side, right_side, (((1,), (1,)), ((), ())), preferred_element_type=F32
    )


def gated(gate_value, up_value):
    return gate_value * jax.nn.sigmoid(gate_value) * up_value


def turn(value, steps):
    size = lax.axis_size("seq")
    return lax.ppermute(value, "seq", [(s, (s - 2 * steps) % size) for s in range(size)])


def swap(value):
    return lax.ppermute(value, "seq", [(s, s ^ 1) for s in range(lax.axis_size("seq"))])


def beside(value, bit):
    return lax.ppermute(value, "fsdp", [(f, f ^ bit) for f in range(lax.axis_size("fsdp"))])


def place():
    own = lax.axis_index("seq")
    return own // 2, own % 2, lax.axis_size("seq") // 2


def tie(value, *others):
    if not others:
        return value
    anywhere = pl.BlockSpec(memory_space=pl.ANY)
    return pl.pallas_call(
        lambda *refs: None,
        out_shape=jax.ShapeDtypeStruct(value.shape, value.dtype),
        in_specs=[anywhere] * (1 + len(others)),
        out_specs=anywhere,
        input_output_aliases={0: 0},
        cost_estimate=pl.CostEstimate(flops=0, bytes_accessed=0, transcendentals=0),
    )(value, *others)


def order(chips):
    near = []
    for step in range(1, chips // 2 + 1):
        near += [step] if 2 * step == chips else [step, chips - step]
    return near


def gather_rows(local):
    return lax.all_gather(local, "seq", axis=0, tiled=True)


def scatter_rows(partial):
    return lax.psum_scatter(partial, "seq", scatter_dimension=0, tiled=True)


def move(kernel, out_shapes, *operands, first=()):
    given = len(operands)
    whole = pl.BlockSpec(memory_space=pltpu.VMEM)
    many = isinstance(out_shapes, tuple)
    moved = sum(x.size * x.dtype.itemsize for x in operands)
    return pl.pallas_call(
        lambda *refs: kernel(*refs[:given], *refs[given + len(first) :]),
        out_shape=out_shapes,
        in_specs=[
            pl.BlockSpec(memory_space=pltpu.SMEM if x.ndim == 1 else pltpu.VMEM)
            for x in operands
        ]
        + [pl.BlockSpec(memory_space=pl.ANY)] * len(first),
        out_specs=tuple([whole] * len(out_shapes)) if many else whole,
        compiler_params=pltpu.CompilerParams(vmem_limit_bytes=48 * 2**20),
        cost_estimate=pl.CostEstimate(flops=0, bytes_accessed=3 * moved, transcendentals=0),
    )(*operands, *first)


def here():
    chip, core, chips = place()
    return jnp.stack([chip, core]).astype(jnp.int32)


def columns_of(weights, blocks, rows_of_extra=()):
    chip, core, chips = place()
    rows = weights[0].shape[0]
    parts = [w.shape[1] // (blocks * 2 * chips) for w in weights]
    cols = blocks * sum(parts) + (128 if rows_of_extra else 0)

    def kernel(at, *refs):
        chip, core = at[0], at[1]
        extra = []
        if rows_of_extra:
            filled = jnp.zeros((rows, 128), F32)
            which = lax.broadcasted_iota(jnp.int32, (rows, 128), 0)
            for i, ref in enumerate(refs[len(parts) : -2]):
                filled = jnp.where(which == i, ref[...], filled)
            extra = [filled.astype(BF)]
        for z in range(chips):
            sides = []
            for c in range(2):
                runs = []
                for ref, part in zip(refs, parts):
                    for b in range(blocks):
                        start = ((b * chips + z) * 2 + c) * part
                        runs.append(ref[:, start : start + part])
                sides.append(jnp.concatenate(runs + extra, axis=1))
            step = (z - chip + chips) % chips
            refs[-2][step] = jnp.where(core == 0, sides[0], sides[1])
            refs[-1][step] = jnp.where(core == 0, sides[1], sides[0])

    side = jax.ShapeDtypeStruct((chips, rows, cols), weights[0].dtype)
    return move(
        kernel,
        (side, side),
        here(),
        *weights,
        *rows_of_extra,
    )


def pairs_of(mine, given, first=()):
    chips = mine.shape[0]

    def kernel(one, two, *outs):
        for step, out in enumerate(outs):
            out[0] = one[step]
            out[1] = two[step]

    pair = jax.ShapeDtypeStruct((2, *mine.shape[1:]), mine.dtype)
    return move(kernel, (pair,) * chips, mine, swap(given), first=first)


def exchange(shares):
    chips = len(shares)
    arrived = {0: shares[0]}
    for step in order(chips):
        arrived[chips - step] = turn(shares[step], -step)
    return [arrived[step] for step in range(chips)]


def rows_of(arrived, first=()):
    chip, core, chips = place()
    pair, rows, cols = arrived[0].shape

    def kernel(at, *refs):
        chip, core = at[0], at[1]
        for step in range(chips):
            for k in range(2):
                refs[-1][(chip + step) % chips, (core + k) % 2] = refs[step][k]

    return move(
        kernel,
        jax.ShapeDtypeStruct((chips, 2, rows, cols), arrived[0].dtype),
        here(),
        *arrived,
        first=first,
    ).reshape(chips * 2 * rows, cols)


def rows_to(summed):
    chip, core, chips = place()
    cols = summed.shape[1]
    rows = summed.shape[0] // (2 * chips)

    def kernel(at, ref, mine, given):
        chip, core = at[0], at[1]
        for step in range(chips):
            mine[step] = ref[(chip + step) % chips, core]
            given[step] = ref[(chip + step) % chips, 1 - core]

    side = jax.ShapeDtypeStruct((chips, rows, cols), summed.dtype)
    return move(
        kernel,
        (side, side),
        here(),
        summed.reshape(chips, 2, rows, cols),
    )


def columns_to(arrived, blocks, widths, first=()):
    chip, core, chips = place()
    pair, rows, cols = arrived[0].shape
    parts = [w // blocks for w in widths]

    def kernel(at, *refs):
        chip, core = at[0], at[1]
        outs = refs[chips:]
        for step in range(chips):
            z = (chip + step) % chips
            at_col = 0
            for out, part in zip(outs, parts):
                for b in range(blocks):
                    one = refs[step][0, :, at_col : at_col + part].astype(F32)
                    two = refs[step][1, :, at_col : at_col + part].astype(F32)
                    both = jnp.concatenate(
                        [jnp.where(core == 0, one, two), jnp.where(core == 0, two, one)], axis=1
                    )
                    start = pl.multiple_of((b * chips + z) * 2 * part, 2 * part)
                    out[:, pl.ds(start, 2 * part)] = both
                    at_col += part

    return move(
        kernel,
        tuple(jax.ShapeDtypeStruct((rows, 2 * chips * w), F32) for w in widths),
        here(),
        *arrived,
        first=first,
    )


def square():
    return lax.axis_size("fsdp") == 4


def flipped(blocks):
    own = lax.axis_index("fsdp")
    odd, high = own % 2 == 1, own // 2 == 1
    a, b, c, d = blocks
    a, b, c, d = (
        jnp.where(odd, b, a),
        jnp.where(odd, a, b),
        jnp.where(odd, d, c),
        jnp.where(odd, c, d),
    )
    return [
        jnp.where(high, c, a),
        jnp.where(high, d, b),
        jnp.where(high, a, c),
        jnp.where(high, b, d),
    ]


def relative_blocks(values):
    if not square():
        return values
    return jnp.concatenate(flipped(jnp.split(values, 4, axis=-1)), axis=-1)


def gather_square(local, ordered=False, first=()):
    if not square():
        return lax.all_gather(local, "fsdp", axis=0, tiled=True), ((), ())
    rows, cols = local.shape
    half = rows // 2
    one = beside(local, 1)
    two = beside(local, 2)
    three = beside(two[:half], 1)
    four = beside(one[half:], 2)

    flip = lax.axis_index("fsdp") if ordered else jnp.int32(0)

    def kernel(at, *refs):
        for i, ref in enumerate(refs[:3]):
            refs[-1][i ^ at[0]] = ref[...]
        refs[-1][3 ^ at[0], :half] = refs[3][...]
        refs[-1][3 ^ at[0], half:] = refs[4][...]

    whole = move(
        kernel,
        jax.ShapeDtypeStruct((4, rows, cols), local.dtype),
        flip.astype(jnp.int32)[None],
        local,
        one,
        two,
        three,
        four,
        first=first,
    )
    return whole.reshape(4 * rows, cols), ((one, two), (three, four))


def weight_terms(rows, grads, blocks, out_rows, turned=(False, False), first=()):
    length = rows.shape[1 if turned[0] else 0]
    cols = grads.shape[0 if turned[1] else 1]

    def kernel(at, rows_ref, grads_ref, *refs):
        contract = (((1,), (1 if turned[1] else 0,)), ((), ()))
        left = rows_ref[...] if turned[0] else rows_ref[...].T
        refs[-1][0] = lax.dot_general(
            left, grads_ref[...], contract, preferred_element_type=F32
        ).astype(BF)

    return pl.pallas_call(
        kernel,
        grid_spec=pltpu.PrefetchScalarGridSpec(
            num_scalar_prefetch=1,
            grid=(blocks.shape[0],),
            in_specs=[
                pl.BlockSpec((out_rows, length), lambda i, at: (at[i], 0))
                if turned[0]
                else pl.BlockSpec((length, out_rows), lambda i, at: (0, at[i])),
                pl.BlockSpec(grads.shape, lambda i, at: (0, 0)),
            ]
            + [pl.BlockSpec(memory_space=pl.ANY)] * len(first),
            out_specs=pl.BlockSpec((1, out_rows, cols), lambda i, at: (i, 0, 0)),
        ),
        out_shape=jax.ShapeDtypeStruct((blocks.shape[0], out_rows, cols), BF),
        compiler_params=pltpu.CompilerParams(vmem_limit_bytes=48 * 2**20),
        cost_estimate=pl.CostEstimate(
            flops=2 * length * out_rows * cols * blocks.shape[0],
            bytes_accessed=2 * (length * (cols + out_rows * blocks.shape[0])),
            transcendentals=0,
        ),
    )(blocks, rows, grads, *first)


def begin_square(rows, grads, ordered=False, turned=(False, False), first=()):
    if not square():
        rows, grads = rows.T if turned[0] else rows, grads.T if turned[1] else grads
        terms = transposed(rows, grads).astype(BF)
        summed = lax.psum_scatter(terms, "fsdp", scatter_dimension=0, tiled=True)
        return lambda *last: (summed,), ()
    half = rows.shape[0 if turned[0] else 1] // 8
    flip = lax.axis_index("fsdp") if ordered else 0

    def terms(which, first):
        at = jnp.stack([2 * (jnp.int32(r) ^ flip) + h for r, h in which]).astype(jnp.int32)
        return weight_terms(rows, grads, at, half, turned, first)

    one = terms([(1, 0), (3, 0)], first)
    two = terms([(2, 1), (3, 1)], first)

    def keep(*last):
        kept = terms([(2, 0), (1, 1), (0, 0), (0, 1)], (one, two, *last))
        return kept, beside(one, 1), beside(two, 2)

    return keep, (one, two)


def begin_square_of(terms, first=()):
    rows, cols = terms.shape
    half = rows // 8

    def kernel(at, g, one, two, kept):
        f = at[0]
        one[0], one[1] = g[1 ^ f, 0], g[3 ^ f, 0]
        two[0], two[1] = g[2 ^ f, 1], g[3 ^ f, 1]
        kept[0], kept[1] = g[2 ^ f, 0], g[1 ^ f, 1]
        kept[2], kept[3] = g[0 ^ f, 0], g[0 ^ f, 1]

    pair = jax.ShapeDtypeStruct((2, half, cols), BF)
    one, two, kept = move(
        kernel,
        (pair, pair, jax.ShapeDtypeStruct((4, half, cols), BF)),
        flip(),
        terms.reshape(4, 2, half, cols),
        first=first,
    )
    return kept, beside(one, 1), beside(two, 2)


def second_square(kept, one=None, two=None, first=()):
    if one is None:
        return (kept,)
    before = first

    def kernel(kept, one, two, first, second):
        first[...] = (kept[0].astype(F32) + one[1].astype(F32)).astype(BF)
        second[...] = (kept[1].astype(F32) + two[1].astype(F32)).astype(BF)

    part = jax.ShapeDtypeStruct(kept.shape[1:], BF)
    first, second = move(kernel, (part, part), kept, one, two, first=before)
    return kept, one, two, beside(first, 2), beside(second, 1)


def finish_square(
    kept, one=None, two=None, one_last=None, two_last=None, kind=BF, first=()
):
    if one is None:
        return kept.astype(kind)

    def kernel(kept, one, two, one_last, two_last, out):
        wide = lambda x: x.astype(F32)
        out[0] = (wide(kept[2]) + wide(one[0]) + wide(one_last[...])).astype(kind)
        out[1] = (wide(kept[3]) + wide(two[0]) + wide(two_last[...])).astype(kind)

    half, cols = kept.shape[1:]
    return move(
        kernel,
        jax.ShapeDtypeStruct((2, half, cols), kind),
        kept,
        one,
        two,
        one_last,
        two_last,
        first=first,
    ).reshape(2 * half, cols)


def turned(values, cosine, sine):
    half = values.shape[0] // 2
    lead, trail = values[:half], values[half:]
    return jnp.concatenate([lead * cosine - trail * sine, trail * cosine + lead * sine], axis=0)


def dot(left_side, right_side):
    return jnp.dot(left_side, right_side, preferred_element_type=F32)


def seen_bias(column_ref, row_ref, bias_ref, block):
    length = row_ref.shape[1]
    for first in range(0, length, block):
        keys = first + block
        ahead = lax.broadcasted_iota(jnp.int32, (keys, block), 0) <= (
            lax.broadcasted_iota(jnp.int32, (keys, block), 1) + first
        )
        same = column_ref[:keys] == row_ref[:, first:keys]
        bias_ref[:keys, first:keys] = jnp.where(same & ahead, 0.0, MASKED)


def attend(qkv, cosine, sine, segment, block, heads, first=()):
    length = qkv.shape[1]
    scale = HD ** (-0.5)

    def kernel(q_ref, k_ref, v_ref, cos_ref, sin_ref, column_ref, row_ref, *refs):
        mixed_ref, query_ref, key_ref, value_ref, log_ref, bias_ref = refs

        @pl.when(pl.program_id(0) == 0)
        def _():
            seen_bias(column_ref, row_ref, bias_ref, block)

        cos, sin = cos_ref[...], sin_ref[...]
        query = turned(q_ref[...], cos, sin).astype(BF) * scale
        key_t = turned(k_ref[...], cos, sin).astype(BF)
        value_t = v_ref[...].astype(BF)
        query_ref[...] = query
        key_ref[...] = key_t
        value_ref[...] = value_t
        key = key_t.T
        for first in range(0, length, block):
            keys = first + block
            scores = dot(key[:keys], query[:, first:keys]) + bias_ref[:keys, first:keys]
            top = jnp.max(scores, axis=0, keepdims=True)
            exponent = jnp.exp(scores - top)
            total = jnp.sum(exponent, axis=0, keepdims=True)
            weights = (exponent * (1.0 / total)).astype(BF)
            mixed_ref[:, first:keys] = dot(value_t[:, :keys], weights).astype(BF)
            log_ref[0, :, first:keys] = top + jnp.log(total)

    head = lambda offset: pl.BlockSpec((HD, length), lambda h: (h + offset, 0))
    whole = pl.BlockSpec(memory_space=pltpu.VMEM)
    tall = jax.ShapeDtypeStruct((heads * HD, length), BF)
    anywhere = pl.BlockSpec(memory_space=pl.ANY)
    return pl.pallas_call(
        lambda *refs: kernel(*refs[:7], *refs[7 + len(first) :]),
        grid=(heads,),
        out_shape=(tall, tall, tall, tall, jax.ShapeDtypeStruct((heads, 1, length), F32)),
        in_specs=[head(0), head(heads), head(2 * heads)]
        + [whole] * 4
        + [anywhere] * len(first),
        out_specs=(
            head(0),
            head(0),
            head(0),
            head(0),
            pl.BlockSpec((1, 1, length), lambda h: (h, 0, 0)),
        ),
        scratch_shapes=[pltpu.VMEM((length, length), F32)],
        compiler_params=pltpu.CompilerParams(vmem_limit_bytes=56 * 2**20),
        cost_estimate=pl.CostEstimate(
            flops=4 * heads * HD * length * length,
            bytes_accessed=24 * heads * HD * length,
            transcendentals=heads * length * length,
        ),
    )(qkv, qkv, qkv, cosine, sine, segment[:, None], segment[None, :], *first)


def attend_back(
    grad, query, key, value, logs, cosine, sine, segment, block, heads, first=()
):
    length = grad.shape[1]
    scale = HD ** (-0.5)

    def kernel(grad_ref, query_ref, key_ref, value_ref, log_ref, *refs):
        cos_ref, sin_ref, column_ref, row_ref, out_ref, bias_ref, key_sum, value_sum = refs

        @pl.when(pl.program_id(0) == 0)
        def _():
            seen_bias(column_ref, row_ref, bias_ref, block)

        cos, sin = cos_ref[...], sin_ref[...]
        grad_t = grad_ref[...]
        query_t, key_t = query_ref[...], key_ref[...]
        grads, queries, key, value = grad_t.T, query_t.T, key_t.T, value_ref[...].T
        for first in reversed(range(0, length, block)):
            keys = first + block
            here_q = slice(first, keys)
            scores = dot(key[:keys], query_t[:, here_q]) + bias_ref[:keys, here_q]
            probs = jnp.exp(scores - log_ref[0, :, here_q])
            grad_probs = dot(value[:keys], grad_t[:, here_q])
            inner = jnp.sum(probs * grad_probs, axis=0, keepdims=True)
            grad_scores = (probs * (grad_probs - inner)).astype(BF)
            key_part = dot(grad_scores, queries[here_q])
            value_part = dot(probs.astype(BF), grads[here_q])
            if keys == length:
                key_sum[...] = key_part
                value_sum[...] = value_part
            else:
                key_sum[:keys] += key_part
                value_sum[:keys] += value_part
            dq = (dot(key_t[:, :keys], grad_scores) * scale).astype(BF).astype(F32)
            out_ref[0, :, here_q] = turned(dq, cos[:, here_q], -sin[:, here_q]).astype(BF)
        dk = key_sum[...].astype(BF).astype(F32).T
        out_ref[1] = turned(dk, cos, -sin).astype(BF)
        out_ref[2] = value_sum[...].T.astype(BF)

    head = pl.BlockSpec((HD, length), lambda h: (h, 0))
    whole = pl.BlockSpec(memory_space=pltpu.VMEM)
    tall = jax.ShapeDtypeStruct((3, heads * HD, length), BF)
    return pl.pallas_call(
        lambda *refs: kernel(*refs[:9], *refs[9 + len(first) :]),
        grid=(heads,),
        out_shape=tall,
        in_specs=[
            head,
            head,
            head,
            head,
            pl.BlockSpec((1, 1, length), lambda h: (h, 0, 0)),
            whole,
            whole,
            whole,
            whole,
        ]
        + [pl.BlockSpec(memory_space=pl.ANY)] * len(first),
        out_specs=pl.BlockSpec((3, HD, length), lambda h: (0, h, 0)),
        scratch_shapes=[
            pltpu.VMEM((length, length), F32),
            pltpu.VMEM((length, HD), F32),
            pltpu.VMEM((length, HD), F32),
        ],
        compiler_params=pltpu.CompilerParams(vmem_limit_bytes=56 * 2**20),
        cost_estimate=pl.CostEstimate(
            flops=10 * heads * HD * length * length,
            bytes_accessed=24 * heads * HD * length,
            transcendentals=heads * length * length,
        ),
    )(grad, query, key, value, logs, cosine, sine, segment[:, None], segment[None, :], *first)


def gain_terms(grads, rows, scales, first=()):
    length, width = rows.shape
    block = 256

    def kernel(grad_ref, row_ref, scale_ref, *refs):
        total = jnp.zeros((1, block), F32)
        step = 256
        for at in range(0, length, step):
            terms = grad_ref[at : at + step].astype(F32) * row_ref[at : at + step].astype(F32)
            total += jnp.sum(terms * scale_ref[at : at + step], axis=0, keepdims=True)
        refs[-1][...] = total

    column = pl.BlockSpec((length, block), lambda i: (0, i))
    return pl.pallas_call(
        kernel,
        grid=(width // block,),
        out_shape=jax.ShapeDtypeStruct((1, width), F32),
        in_specs=[
            column,
            column,
            pl.BlockSpec((length, 1), lambda i: (0, 0)),
        ]
        + [pl.BlockSpec(memory_space=pl.ANY)] * len(first),
        out_specs=pl.BlockSpec((1, block), lambda i: (0, i)),
        cost_estimate=pl.CostEstimate(
            flops=4 * length * width, bytes_accessed=4 * length * width, transcendentals=0
        ),
    )(grads, rows, scales, *first).reshape(width)


def mlp(rows, gate_up_weight, down_full):
    length, width = rows.shape
    hidden_width = down_full.shape[0]
    tall, block, wide = min(1024, length), min(256, hidden_width), 512
    steps, ends = hidden_width // block, width // wide

    def kernel(x_ref, gate_w, up_w, down_w, gate_ref, up_ref, hidden_ref, out_ref, kept):
        step = pl.program_id(1)

        @pl.when(step < steps)
        def _():
            x = x_ref[...]
            gate, up = dot(x, gate_w[...]), dot(x, up_w[...])
            hidden = gated(gate, up).astype(BF)
            gate_ref[...], up_ref[...], hidden_ref[...] = gate, up, hidden
            kept[jnp.minimum(step, steps - 1)] = hidden

        @pl.when(step >= steps)
        def _():
            hidden = jnp.concatenate([kept[i] for i in range(steps)], axis=1)
            out_ref[...] = dot(hidden, down_w[...]).astype(BF)

    early = lambda j: jnp.minimum(j, steps - 1)
    late = lambda j: jnp.maximum(j - steps, 0)
    part = pl.BlockSpec((tall, block), lambda i, j: (i, early(j)))
    full = jax.ShapeDtypeStruct((length, hidden_width), F32)
    return pl.pallas_call(
        kernel,
        grid=(length // tall, steps + ends),
        out_shape=(
            full,
            full,
            jax.ShapeDtypeStruct((length, hidden_width), BF),
            jax.ShapeDtypeStruct((length, width), BF),
        ),
        in_specs=[
            pl.BlockSpec((tall, width), lambda i, j: (i, 0)),
            pl.BlockSpec((width, block), lambda i, j: (0, early(j))),
            pl.BlockSpec((width, block), lambda i, j: (0, early(j) + steps)),
            pl.BlockSpec((hidden_width, wide), lambda i, j: (0, late(j))),
        ],
        out_specs=(part, part, part, pl.BlockSpec((tall, wide), lambda i, j: (i, late(j)))),
        scratch_shapes=[pltpu.VMEM((steps, tall, block), BF)],
        compiler_params=pltpu.CompilerParams(vmem_limit_bytes=56 * 2**20),
        cost_estimate=pl.CostEstimate(
            flops=6 * length * width * hidden_width,
            bytes_accessed=6 * width * hidden_width + 4 * length * (width + 3 * hidden_width),
            transcendentals=length * hidden_width,
        ),
    )(rows, gate_up_weight, gate_up_weight, down_full)


def mlp_back(grads, gate, up, gate_up_weight, down_full):
    length, width = grads.shape
    hidden_width = down_full.shape[0]
    tall, block, wide = min(1024, length), min(256, hidden_width), 512
    steps, ends = hidden_width // block, width // wide

    def kernel(g_ref, gate_ref, up_ref, down_w, both_w, dgate, dup, out_ref, kept):
        step = pl.program_id(1)

        @pl.when(step < steps)
        def _():
            gate, up = gate_ref[...], up_ref[...]
            share = jax.nn.sigmoid(gate)
            grad_hidden = against(g_ref[...], down_w[...])
            grad_gate = (grad_hidden * up * (share + gate * share * (1.0 - share))).astype(BF)
            grad_up = (grad_hidden * (gate * share)).astype(BF)
            dgate[...], dup[...] = grad_gate, grad_up
            at = jnp.minimum(step, steps - 1)
            kept[at] = grad_gate
            kept[at + steps] = grad_up

        @pl.when(step >= steps)
        def _():
            both = jnp.concatenate([kept[i] for i in range(2 * steps)], axis=1)
            out_ref[...] = against(both, both_w[...]).astype(BF)

    early = lambda j: jnp.minimum(j, steps - 1)
    late = lambda j: jnp.maximum(j - steps, 0)
    part = pl.BlockSpec((tall, block), lambda i, j: (i, early(j)))
    narrow = jax.ShapeDtypeStruct((length, hidden_width), BF)
    return pl.pallas_call(
        kernel,
        grid=(length // tall, steps + ends),
        out_shape=(narrow, narrow, jax.ShapeDtypeStruct((length, width), BF)),
        in_specs=[
            pl.BlockSpec((tall, width), lambda i, j: (i, 0)),
            part,
            part,
            pl.BlockSpec((block, width), lambda i, j: (early(j), 0)),
            pl.BlockSpec((wide, 2 * hidden_width), lambda i, j: (late(j), 0)),
        ],
        out_specs=(part, part, pl.BlockSpec((tall, wide), lambda i, j: (i, late(j)))),
        scratch_shapes=[pltpu.VMEM((2 * steps, tall, block), BF)],
        compiler_params=pltpu.CompilerParams(vmem_limit_bytes=56 * 2**20),
        cost_estimate=pl.CostEstimate(
            flops=6 * length * width * hidden_width,
            bytes_accessed=6 * width * hidden_width + 4 * length * (width + 3 * hidden_width),
            transcendentals=length * hidden_width,
        ),
    )(grads, gate, up, down_full, gate_up_weight)


def rows_back(columns, weight, first=()):
    inner, length = columns.shape
    rows = columns.T
    width = weight.shape[0]
    block = 512

    def kernel(rows_ref, weight_ref, *refs):
        refs[-1][...] = against(rows_ref[...], weight_ref[...]).astype(BF)

    return pl.pallas_call(
        kernel,
        grid=(width // block,),
        out_shape=jax.ShapeDtypeStruct((length, width), BF),
        in_specs=[
            pl.BlockSpec((length, inner), lambda j: (0, 0)),
            pl.BlockSpec((block, inner), lambda j: (j, 0)),
        ]
        + [pl.BlockSpec(memory_space=pl.ANY)] * len(first),
        out_specs=pl.BlockSpec((length, block), lambda j: (0, j)),
        compiler_params=pltpu.CompilerParams(vmem_limit_bytes=48 * 2**20),
        cost_estimate=pl.CostEstimate(
            flops=2 * length * width * inner,
            bytes_accessed=2 * (length * (width + inner) + width * inner),
            transcendentals=0,
        ),
    )(rows, weight, *first)


def flip():
    return (lax.axis_index("fsdp") if square() else jnp.int32(0)).astype(jnp.int32)[None]


def spots(at, width):
    size = width // 4
    return [pl.ds(pl.multiple_of((g ^ at[0]) * size, size), size) for g in range(4)]


def steadied(values):
    return lax.rsqrt(jnp.mean(values * values, axis=-1, keepdims=True) + EPSILON)


def after_first_sum(summed, tokens, gain, first):
    rows, width = tokens.shape

    def kernel(at, summed_ref, tokens_ref, gain_ref, attended_ref, normed_ref):
        values = tokens_ref[...].astype(F32) + summed_ref[...].astype(F32)
        attended_ref[...] = values
        normed = (values * steadied(values) * gain_ref[...]).astype(BF)
        for g, spot in enumerate(spots(at, width)):
            normed_ref[:, spot] = normed[:, g * (width // 4) : (g + 1) * (width // 4)]

    return move(
        kernel,
        (
            jax.ShapeDtypeStruct((rows, width), F32),
            jax.ShapeDtypeStruct((rows, width), BF),
        ),
        flip(),
        summed,
        tokens,
        gain[None, :],
        first=first,
    )


def after_second_sum(summed, attended, teacher, mask, weight):
    rows, width = attended.shape

    def kernel(summed_ref, attended_ref, teacher_ref, mask_ref, weight_ref, *outs):
        out_ref, grad_ref, low_ref, error_ref = outs
        result = attended_ref[...] + summed_ref[...].astype(F32)
        difference = result - teacher_ref[...].astype(F32)
        out_ref[...] = result.astype(BF)
        grad = weight_ref[...] * difference
        grad_ref[...] = grad
        low_ref[...] = grad.astype(BF)
        terms = jnp.sum(mask_ref[...] * difference * difference, axis=0, keepdims=True)
        error_ref[...] = jnp.broadcast_to(jnp.sum(terms, axis=1, keepdims=True), (1, 128))

    narrow = jax.ShapeDtypeStruct((rows, width), BF)
    wide = jax.ShapeDtypeStruct((rows, width), F32)
    return move(
        kernel,
        (narrow, wide, narrow, jax.ShapeDtypeStruct((1, 128), F32)),
        summed,
        attended,
        teacher,
        mask,
        weight,
    )


def after_third_sum(summed, attended, gain, grad_result, first):
    rows, width = attended.shape

    def kernel(at, summed_ref, attended_ref, gain_ref, result_ref, wide_ref, low_ref, gain_out):
        grads = jnp.concatenate([summed_ref[:, spot] for spot in spots(at, width)], axis=1)
        grads = grads.astype(F32)
        values = attended_ref[...]
        steady = steadied(values)
        gain_out[...] = jnp.sum(grads * values * steady, axis=0, keepdims=True)
        scaled = grads * gain_ref[...]
        inner = jnp.mean(scaled * values, axis=-1, keepdims=True)
        total = result_ref[...] + steady * scaled - values * (steady * steady * steady * inner)
        wide_ref[...] = total
        low_ref[...] = total.astype(BF)

    return move(
        kernel,
        (
            jax.ShapeDtypeStruct((rows, width), F32),
            jax.ShapeDtypeStruct((rows, width), BF),
            jax.ShapeDtypeStruct((1, width), F32),
        ),
        flip(),
        summed,
        attended,
        gain[None, :],
        grad_result,
        first=first,
    )


def after_last_sum(summed, tokens, gain, grad_after):
    rows, width = tokens.shape

    def kernel(at, summed_ref, tokens_ref, gain_ref, after_ref, out_ref):
        grads = jnp.concatenate([summed_ref[:, spot] for spot in spots(at, width)], axis=1)
        values = tokens_ref[...].astype(F32)
        steady = steadied(values)
        scaled = grads.astype(F32) * gain_ref[...]
        inner = jnp.mean(scaled * values, axis=-1, keepdims=True)
        out_ref[...] = (
            after_ref[...] + steady * scaled - values * (steady * steady * steady * inner)
        )

    return move(
        kernel,
        jax.ShapeDtypeStruct((rows, width), F32),
        flip(),
        summed,
        tokens,
        gain[None, :],
        grad_after,
    )


def sum_to_owners(values):
    chip, core, chips = place()
    shards, width = lax.axis_size("fsdp"), values.shape[1]
    own = lax.axis_index("fsdp")

    def share(values, at):
        return lax.dynamic_index_in_dim(values, at, 0, keepdims=False)

    values = values.reshape(shards, chips, 2, width)
    total = share(values, own)
    for step in range(1, shards):
        total += lax.ppermute(
            share(values, (own + step) % shards),
            "fsdp",
            [(f, (f + step) % shards) for f in range(shards)],
        )
    total = jnp.moveaxis(total, 1, 0)
    values = share(total, core) + swap(share(total, 1 - core))
    total = share(values, chip)
    for step in order(chips):
        total += turn(share(values, (chip + step) % chips), -step)
    return total


def body(
    tokens,
    teacher,
    segments,
    valid,
    query_weight,
    key_weight,
    value_weight,
    output_weight,
    attention_gain,
    gate_weight,
    up_weight,
    down_weight,
    mlp_gain,
):
    sequences, local_rows, width = tokens.shape
    groups = lax.axis_size("seq")
    shards = lax.axis_size("fsdp")
    heads = H // groups
    length = local_rows * groups
    own = lax.axis_index("seq")
    chip, core, chips = place()
    weight_rows = query_weight.shape[0]
    aligned = H % (shards * groups) == 0
    head_blocks = shards if aligned else 1
    hw = heads * HD

    own_tokens = tokens.reshape(local_rows, width)
    keep_mask = valid.reshape(local_rows).astype(F32)
    lane_pad = lambda row: jnp.pad(row, ((0, 0), (0, 128 - row.shape[1])))
    own_gains = jnp.concatenate([attention_gain, mlp_gain])[None, :]
    extra_rows = (
        lane_pad(own_gains.astype(F32)),
        lane_pad((segments // 256).astype(F32)),
        lane_pad((segments % 256).astype(F32)),
        jnp.broadcast_to(jnp.sum(keep_mask), (1, 128)),
    )
    attention_shares = exchange(
        pairs_of(
            *columns_of([query_weight, key_weight, value_weight], head_blocks, extra_rows)
        )
    )
    if aligned:
        out_weight = lax.all_gather(output_weight, "fsdp", axis=0, tiled=True)
    else:
        out_weight = lax.dynamic_slice_in_dim(
            lax.all_gather(output_weight, ALL, axis=0, tiled=True), own * hw, hw, 0
        )
    down_full, down_steps = gather_square(down_weight, ordered=True)
    tokens_all = gather_rows(
        tie(relative_blocks(own_tokens), *attention_shares[1:], out_weight, *down_steps[0])
    )
    gate_up_shares = exchange(
        pairs_of(*columns_of([gate_weight, up_weight], shards), first=attention_shares[1:])
    )
    attention_in = gather_square(rows_of(attention_shares))[0]
    gate_up_weight, gate_up_steps = gather_square(rows_of(gate_up_shares))

    qkv_weight = attention_in[:, : 3 * hw]
    extras = attention_in[:, 3 * hw :].reshape(shards * groups, weight_rows, 128).astype(F32)
    normed_gain = extras[:, 0, :weight_rows].reshape(width)
    gains = relative_blocks(
        jnp.stack([normed_gain, extras[:, 0, weight_rows : 2 * weight_rows].reshape(width)])
    )
    first_gain, second_gain = gains[0], gains[1]
    count = jnp.sum(extras[:, 3, 0])
    table = lax.dynamic_slice_in_dim(
        extras, 0 if square() else lax.axis_index("fsdp") * groups, groups, 0
    ).astype(jnp.int32)
    segment = (table[:, 1, :local_rows] * 256 + table[:, 2, :local_rows]).reshape(length)
    cosine, sine = rope_tables(length)

    wide_tokens = tokens_all.astype(F32)
    steady = lax.rsqrt(jnp.mean(wide_tokens * wide_tokens, axis=-1, keepdims=True) + EPSILON)
    normed = (wide_tokens * steady * normed_gain).astype(BF)
    qkv = lax.dot_general(
        qkv_weight, normed, (((0,), (1,)), ((), ())), preferred_element_type=F32
    )
    mixed, query, key, value, logs = attend(
        qkv, cosine, sine, segment, 2 * local_rows, heads, first=(gate_up_shares[-1],)
    )
    mixed = tie(mixed, *gate_up_shares[1:], *down_steps[1])
    after_attention, normed_two = after_first_sum(
        scatter_rows(transposed(mixed, out_weight).astype(BF)),
        own_tokens,
        second_gain,
        gate_up_steps[0],
    )
    normed_two = gather_rows(normed_two)
    gate_value, up_value, hidden, partial = mlp(normed_two, gate_up_weight, down_full)
    hidden_width = hidden.shape[1]
    output, grad_result, grad_branch, error_sum = after_second_sum(
        scatter_rows(partial),
        after_attention,
        teacher.reshape(local_rows, width),
        keep_mask[:, None],
        (2.0 / count * keep_mask)[:, None],
    )
    grad_branch = gather_rows(grad_branch)
    grad_gate, grad_upward, grad_normed_sum = mlp_back(
        grad_branch, gate_value, up_value, gate_up_weight, down_full
    )
    gate_keep, unused = begin_square(normed_two, grad_gate, first=(grad_normed_sum,))
    gate_back = gate_keep()
    up_keep, unused = begin_square(normed_two, grad_upward, first=gate_back[:1])
    up_back = up_keep(*gate_back[1:])
    grad_after, grad_out, second_gain_grad = after_third_sum(
        scatter_rows(grad_normed_sum),
        after_attention,
        second_gain,
        grad_result,
        up_back,
    )
    gate_back = second_square(*gate_back)

    grad_out = gather_rows(grad_out)
    up_back = second_square(*up_back)
    down_keep, down_sent = begin_square(hidden, grad_branch, ordered=True, first=gate_back[:1])
    down_back = down_keep()
    gate_up_pairs = pairs_of(
        *rows_to(
            jnp.concatenate(
                [
                    finish_square(*gate_back, first=down_sent),
                    finish_square(*up_back, first=down_back[:1]),
                ],
                axis=1,
            )
        )
    )
    gate_up_shares = exchange(gate_up_pairs)
    grad_mixed = against(out_weight, grad_out).astype(BF)
    qkv_grad = attend_back(
        grad_mixed,
        query,
        key,
        value,
        logs,
        cosine,
        sine,
        segment,
        2 * local_rows,
        heads,
        first=gate_up_pairs,
    ).reshape(3 * hw, length)
    down_back = second_square(*down_back, first=gate_up_pairs)
    grad_normed_sum = rows_back(
        qkv_grad, attention_in, (*gate_up_shares[1:], *down_back[3:])
    )
    qkv_keep, qkv_sent = begin_square(
        normed, qkv_grad, turned=(False, True), first=(grad_normed_sum,)
    )
    first_gain_grad = gain_terms(grad_normed_sum, tokens_all, steady, qkv_sent)
    qkv_begun = qkv_keep(first_gain_grad)
    output_grad = matmul(mixed, grad_out).astype(BF)
    if aligned and square():
        output_begun = begin_square_of(output_grad, first=qkv_begun[:1])
        qkv_back = second_square(*qkv_begun, first=output_begun[:1])
        output_back = second_square(*output_begun)
        output_sum = finish_square(*output_back, kind=F32)
    else:
        qkv_back = second_square(*qkv_begun)
        output_begun = ()
        output_sum = lax.psum_scatter(
            lax.dynamic_update_slice_in_dim(
                jnp.zeros((width, width), BF), output_grad, own * hw, 0
            ),
            ALL,
            scatter_dimension=0,
            tiled=True,
        ).astype(F32)
    devices = shards * groups
    sums = sum_to_owners(
        jnp.concatenate(
            [
                relative_blocks(first_gain_grad).reshape(devices, weight_rows),
                second_gain_grad.reshape(devices, weight_rows),
                jnp.broadcast_to(error_sum, (devices, 128)),
            ],
            axis=1,
        )
    )
    qkv_pairs = pairs_of(
        *rows_to(finish_square(*qkv_back)), first=(sums, *output_begun[1:])
    )
    qkv_shares = exchange(qkv_pairs)
    gate_sum, up_sum = columns_to(
        gate_up_shares, shards, [hidden_width, hidden_width], first=qkv_back[3:4]
    )
    down_sum = finish_square(*down_back, kind=F32, first=qkv_back[3:4])
    grad_inputs = after_last_sum(
        scatter_rows(grad_normed_sum), own_tokens, first_gain, grad_after
    )
    query_sum, key_sum, value_sum = columns_to(
        qkv_shares,
        head_blocks,
        [hw, hw, hw],
        first=(gate_sum, down_sum, grad_inputs, output_sum),
    )
    output_shape = (sequences, local_rows, width)
    return (
        output.reshape(output_shape),
        sums[2 * weight_rows] / count,
        grad_inputs.reshape(output_shape),
        query_sum,
        key_sum,
        value_sum,
        output_sum,
        sums[:weight_rows],
        gate_sum,
        up_sum,
        down_sum,
        sums[weight_rows : 2 * weight_rows],
    )


def solution(mesh):
    rows = P("fsdp", "seq", None)
    places = P("fsdp", "seq")
    matrix = P(ALL, None)
    vector = P(ALL)
    return jax.shard_map(
        body,
        mesh=mesh,
        in_specs=(
            rows,
            rows,
            places,
            places,
            matrix,
            matrix,
            matrix,
            matrix,
            vector,
            matrix,
            matrix,
            matrix,
            vector,
        ),
        out_specs=(
            rows,
            P(),
            rows,
            matrix,
            matrix,
            matrix,
            matrix,
            vector,
            matrix,
            matrix,
            matrix,
            vector,
        ),
        check_vma=False,
    )
```
